256 devices in a mesh: dir: 8 (over x, core), surf: 32 (over y, z).
Axes of the slice: x: 4, y: 4, z: 8, core: 2. Of those that a mesh axis runs over, the one named last changes fastest.
Arguments:
- direction_angles: float32 [2, 32768], P(None, 'dir'), may hold values from -3.140625 to 3.140625
- positions: float32 [3, 24576], P(None, 'surf'), may hold values from -12 to 12
- normal_angles: float32 [2, 24576], P(None, 'surf'), may hold values from -3.140625 to 3.140625
- areas: float32 [24576], P('surf'), may hold values from 0.5 to 2
- pressure: bfloat16 [24576, 128], P('surf'), may hold values from -6 to 6
- velocity: bfloat16 [24576, 128], P('surf'), may hold values from -6 to 6
- targets: float32 [32768, 64], P('dir'), may hold values from 0.5 to 3
Outputs:
- responses: float32 [32768, 128], P(('dir', 'surf'))
- grad_pressure: float32 [24576, 128], P('surf')
- grad_velocity: float32 [24576, 128], P('surf')
The draws below stay inside these ranges and needn't reach their ends.
All inputs are finite; a program needn't handle non-finite values.
Results may differ from the reference program's by a relative error of at most 0.0052.
Values may be sent and summed in bfloat16 or wider, within the bound.
A program may use at most 64 MiB of HBM per device.

```python
import math
import jax
import jax.numpy as jnp
from jax import lax

CASES = 64
DIRS = 32768
PATCHES = 24576


def level_of(own_key, extent, shards, least, top_value):
    factor_of = 1.0
    for axis_at, parts in shards:
        draws = jax.random.uniform(jax.random.fold_in(jax.random.fold_in(own_key, 6), axis_at), (parts,), jnp.float32, least / len(shards), top_value / len(shards))
        factor_of = factor_of * jnp.repeat(jnp.exp(draws), extent[axis_at] // parts).reshape((-1,) + (1,) * (len(extent) - 1 - axis_at))
    return factor_of


def gaussian(key, extent, spread, reach, split=(), held_as=jnp.bfloat16):
    factor_of = level_of(key, extent, split, -0.22, 0.18) if split else 1.0
    drawn = jax.random.normal(key, extent, jnp.float32) * spread * factor_of
    return jnp.minimum(jnp.maximum(drawn, -reach), reach).astype(held_as)


def setup_inputs(seed: int = 0) -> dict:
    key_list = jax.random.split(jax.random.key(seed), 8)
    return {
        "direction_angles": jnp.clip(jax.random.uniform(key_list[0], (2, DIRS), jnp.float32, -3.140625, 3.140625), -3.140625, 3.140625),
        "positions": jnp.clip(jax.random.uniform(key_list[1], (3, PATCHES), jnp.float32, -12.0, 12.0) * level_of(key_list[1], (3, PATCHES), ((1, 32),), -0.4, 0.0), -12.0, 12.0),
        "normal_angles": jnp.clip(jax.random.uniform(key_list[2], (2, PATCHES), jnp.float32, -3.140625, 3.140625), -3.140625, 3.140625),
        "areas": jnp.clip(jnp.exp(math.log(2.0) - 1.3862944 * jax.random.uniform(key_list[3], (PATCHES,), jnp.float32) ** level_of(key_list[3], (PATCHES,), ((0, 32),), -0.2, 0.2)), 0.5, 2.0),
        "pressure": gaussian(key_list[4], (PATCHES, 2 * CASES), 1.0, 6.0, ((0, 32),)),
        "velocity": gaussian(key_list[5], (PATCHES, 2 * CASES), 1.0, 6.0, ((0, 32),)),
        "targets": jnp.clip(0.5 + 2.5 * jax.random.uniform(key_list[6], (DIRS, CASES), jnp.float32) ** level_of(key_list[6], (DIRS, CASES), ((0, 8),), -0.2, 0.2), 0.5, 3.0),
    }


floor_value = 0.5

def unit_vectors(angles):
    polar = angles[0]
    azimuth = angles[1]
    return jnp.stack([jnp.sin(polar) * jnp.cos(azimuth), jnp.sin(polar) * jnp.sin(azimuth), jnp.cos(polar)])

def kernel_tile(toward, points, facing):
    phase_angle = toward[0][:, None] * points[0][None, :] + toward[1][:, None] * points[1][None, :] + toward[2][:, None] * points[2][None, :]
    alignment = toward[0][:, None] * facing[0][None, :] + toward[1][:, None] * facing[1][None, :] + toward[2][:, None] * facing[2][None, :]
    cosine = jnp.cos(phase_angle)
    sine_part = jnp.sin(phase_angle)
    return jnp.concatenate([cosine.astype(jnp.bfloat16), (-sine_part).astype(jnp.bfloat16), (cosine * alignment).astype(jnp.bfloat16), (-sine_part * alignment).astype(jnp.bfloat16)], axis=1)

def stacked_sources(weighted_v, weighted_p, cases):
    velocity_real = weighted_v[:, :cases]
    velocity_imag = weighted_v[:, cases:]
    pressure_real = weighted_p[:, :cases]
    pressure_imag = weighted_p[:, cases:]
    return jnp.concatenate([weighted_v, jnp.concatenate([-velocity_imag, velocity_real], 1), weighted_p, jnp.concatenate([-pressure_imag, pressure_real], 1)], 0)

def misfit_residual(responses, targets):
    cases = targets.shape[1]
    real_part = responses[:, :cases]
    imag_part = responses[:, cases:]
    magnitude = jnp.sqrt(real_part * real_part + imag_part * imag_part)
    weight = (magnitude - targets) / jnp.maximum(magnitude, floor_value)
    return jnp.concatenate([weight * real_part, weight * imag_part], 1).astype(jnp.bfloat16)

def combine_terms(products, scales, patch_rows, cases):
    mono_a = products[:patch_rows]
    mono_b = products[patch_rows:2 * patch_rows]
    dip_a = products[2 * patch_rows:3 * patch_rows]
    dip_b = products[3 * patch_rows:]
    mono_real = mono_a[:, :cases] + mono_b[:, cases:]
    mono_imag = mono_a[:, cases:] - mono_b[:, :cases]
    dip_real = dip_a[:, :cases] + dip_b[:, cases:]
    dip_imag = dip_a[:, cases:] - dip_b[:, :cases]
    column = scales[:, None]
    return jnp.concatenate([column * dip_imag, -column * dip_real, column * mono_imag, -column * mono_real], 1)

def reference(direction_angles, positions, normal_angles, areas, pressure, velocity, targets):
    toward = unit_vectors(direction_angles)
    facing = unit_vectors(normal_angles)
    scales = areas * jnp.float32(1.0 / math.sqrt(PATCHES))
    weighted_p = (pressure.astype(jnp.float32) * scales[:, None]).astype(jnp.bfloat16)
    weighted_v = (velocity.astype(jnp.float32) * scales[:, None]).astype(jnp.bfloat16)
    stacked = stacked_sources(weighted_v, weighted_p, CASES).astype(jnp.float32)
    block_rows = math.gcd(DIRS, 256)
    block_count = DIRS // block_rows

    def forward_block(block_index):
        dir_rows = lax.dynamic_slice_in_dim(toward, block_index * block_rows, block_rows, 1)
        kernel = kernel_tile(dir_rows, positions, facing).astype(jnp.float32)
        return jnp.dot(kernel, stacked, precision=lax.Precision.HIGHEST, preferred_element_type=jnp.float32)
    totals = lax.map(forward_block, jnp.arange(block_count, dtype=jnp.int32)).reshape(DIRS, 2 * CASES)
    responses = jnp.concatenate([-totals[:, CASES:], totals[:, :CASES]], 1)
    residual = misfit_residual(responses, targets)

    def adjoint_step(running, block_index):
        dir_rows = lax.dynamic_slice_in_dim(toward, block_index * block_rows, block_rows, 1)
        kernel = kernel_tile(dir_rows, positions, facing).astype(jnp.float32)
        res_rows = lax.dynamic_slice_in_dim(residual, block_index * block_rows, block_rows, 0).astype(jnp.float32)
        part_sum = lax.dot_general(kernel, res_rows, (((0,), (0,)), ((), ())), precision=lax.Precision.HIGHEST, preferred_element_type=jnp.float32)
        return (running + part_sum, None)
    initial = jnp.zeros((4 * PATCHES, 2 * CASES), jnp.float32)
    adjoint, unused = lax.scan(adjoint_step, initial, jnp.arange(block_count, dtype=jnp.int32))
    gradients = combine_terms(adjoint, scales, PATCHES, CASES)
    return (responses, gradients[:, :2 * CASES], gradients[:, 2 * CASES:])
```

```python
import functools
import math

import jax
import jax.numpy as jnp
from jax import lax
from jax.experimental import pallas as pl
from jax.experimental.pallas import tpu as pltpu
from jax.sharding import PartitionSpec as P

MESH = pl.DeviceIdType.MESH
BF = jnp.bfloat16
F32 = jnp.float32
FLOOR = 0.5

TILES = 4
NY, NZ, NX = 4, 8, 4
OWN = 32
SUB = NZ * OWN
ROWS = NY * SUB
DELTAS = (2, 1, 3, 0)
SLOT_OF_SEND = {1: 2, 2: 0, 3: 1}

ROOT2 = math.sqrt(2.0)
SIN_HALF = [c * ROOT2 for c in (3.14158198, -5.1671413, 2.54188707, -0.55460885)]
COS_HALF = [c * ROOT2 for c in (0.99999325, -4.93393467, 4.0412481, -1.22203176)]
SIN_FINE = [c * ROOT2 for c in (3.14159258, -5.16770687, 2.55003119, -0.59804419, 0.07721839)]
COS_FINE = [c * ROOT2 for c in (0.99999995, -4.93479283, 4.05841135, -1.33187657, 0.21968961)]


def horner(coefficients, square):
    value = coefficients[-1]
    for coefficient in coefficients[-2::-1]:
        value = value * square + coefficient
    return value


def cos_sin(cycles, sin_half, cos_half):
    rest = cycles - jnp.round(cycles)
    square = rest * rest
    half_sine = horner(sin_half, square) * rest
    half_cosine = horner(cos_half, square)
    return 1.0 - half_sine * half_sine, half_sine * half_cosine


def fine_cos_sin(angle):
    return cos_sin(angle * F32(1.0 / (2.0 * math.pi)), SIN_FINE, COS_FINE)


def unit_rows(angles):
    cos_all, sin_all = fine_cos_sin(angles)
    cos_polar, sin_polar = cos_all[0:1], sin_all[0:1]
    cos_azimuth, sin_azimuth = cos_all[1:2], sin_all[1:2]
    return sin_polar * cos_azimuth, sin_polar * sin_azimuth, cos_polar


def three_parts(value):
    first = value.astype(BF).astype(F32)
    second = (value - first).astype(BF).astype(F32)
    return first, second, value - first - second


def body(
    total_patches,
    angles_ref, positions_ref, normals_ref, areas_ref, pressure_ref, velocity_ref, targets_hbm,
    responses_ref, grad_p_ref, grad_v_ref,
    targets_ref, split_t, split_x, t_rows, t_cols, t_lhs, x_rhs, face_rows, weights,
    cos_a, sin_a, cos_b, sin_b,
    part_send, part_own, part_recv, row_own, row_send, row_recv, res_all, acc,
    half_send, half_recv, quarter_own, quarter_send, quarter_recv, grad_all,
    local_sem, a_send, a_recv, b_send, b_recv, d_send, d_recv, e_send, e_recv,
    g_send, g_recv, h_send, h_recv, k_send, k_recv,
):
    dir_index = lax.axis_index("dir")
    surf_index = lax.axis_index("surf")
    x, core = dir_index // 2, lax.rem(dir_index, 2)
    y, z = surf_index // NZ, lax.rem(surf_index, NZ)
    patches = positions_ref.shape[1]

    def at_y(e):
        return (dir_index, lax.rem(y + e, NY) * NZ + z)

    def at_z(e):
        return (dir_index, y * NZ + lax.rem(z + e, NZ))

    def at_dir(ex, ec):
        return (lax.rem(x + ex, NX) * 2 + lax.rem(core + ec, 2), surf_index)

    group = [(ex, ec) for ex in range(NX) for ec in range(2) if ex or ec]
    barrier = pltpu.get_barrier_semaphore()
    for e in range(1, NY):
        pl.semaphore_signal(barrier, inc=1, device_id=at_y(e), device_id_type=MESH)
    for e in range(1, NZ):
        pl.semaphore_signal(barrier, inc=1, device_id=at_z(e), device_id_type=MESH)
    for ex, ec in group:
        pl.semaphore_signal(barrier, inc=1, device_id=at_dir(ex, ec), device_id_type=MESH)

    own_rows = TILES * OWN
    fetch = pltpu.make_async_copy(
        targets_hbm.at[pl.ds(pl.multiple_of(surf_index * own_rows, own_rows), own_rows)],
        targets_ref, local_sem,
    )
    fetch.start()

    tx, ty, tz = unit_rows(angles_ref[...])
    split_t[...] = jnp.zeros_like(split_t)
    split_x[...] = jnp.zeros_like(split_x)
    t_rows[...] = jnp.zeros_like(t_rows)
    for k, row in enumerate((tx, ty, tz)):
        t_rows[k : k + 1, :] = row
        first, second, third = three_parts(row)
        for at, part in enumerate((first, first, second, second, first, third)):
            split_t[3 * at + k : 3 * at + k + 1, :] = part
        first, second, third = three_parts(positions_ref[k : k + 1, :] * F32(0.5 / math.pi))
        for at, part in enumerate((first, second, first, second, third, first)):
            split_x[3 * at + k : 3 * at + k + 1, :] = part
    x_rhs[...] = split_x[...].astype(BF)
    t_lhs[...] = split_t[...].T.astype(BF)
    t_cols[...] = t_rows[...].T

    face_rows[...] = jnp.zeros_like(face_rows)
    scale_row = areas_ref[...] * F32(1.0 / math.sqrt(total_patches))
    for k, row in enumerate(unit_rows(normals_ref[...])):
        face_rows[k : k + 1, :] = row
    face_rows[3:4, :] = scale_row
    face_cols = face_rows[...].T
    scale_col = face_cols[:, 3:4]
    weighted_p = (pressure_ref[...].astype(F32) * scale_col).astype(BF).astype(F32)
    weighted_v = (velocity_ref[...].astype(F32) * scale_col).astype(BF).astype(F32)
    cases = weighted_p.shape[1] // 2
    for k in range(4):
        source = weighted_v if k == 0 else weighted_p * face_cols[:, k - 1 : k]
        turned = jnp.concatenate([source[:, cases:], -source[:, :cases]], axis=1)
        columns = slice(k * 2 * cases, (k + 1) * 2 * cases)
        weights[0:patches, columns] = source.astype(BF)
        weights[patches : 2 * patches, columns] = turned.astype(BF)
    acc[...] = jnp.zeros_like(acc)

    def sub_row(q, j):
        return pl.multiple_of(q * ROWS + lax.rem(y + DELTAS[j], NY) * SUB, SUB)

    def trig_piece(q, j, cos_ref, sin_ref, slot, begin, count):
        angle = jnp.dot(
            t_lhs[pl.ds(sub_row(q, j) + begin, count), :], x_rhs[...], preferred_element_type=F32
        )
        cosine, sine = cos_sin(angle, SIN_HALF, COS_HALF)
        at = pl.multiple_of(slot * SUB + begin, count)
        cos_ref[pl.ds(at, count), :] = cosine.astype(BF)
        sin_ref[pl.ds(at, count), :] = sine.astype(BF)

    quarter = SUB // 4

    def forward_step(tq, tj, tslot, mq, mj, mslot):
        tc, ts = (cos_a, sin_a) if tj % 2 == 0 else (cos_b, sin_b)
        mc, ms = (cos_a, sin_a) if mj % 2 == 0 else (cos_b, sin_b)
        rows = pl.ds(pl.multiple_of(mslot * SUB, SUB), SUB)
        halves = []
        for h in range(2):
            columns = slice(4 * cases * h, 4 * cases * (h + 1))
            g = jnp.dot(mc[rows, :], weights[0:patches, columns], preferred_element_type=F32)
            trig_piece(tq, tj, tc, ts, tslot, 2 * h * quarter, quarter)
            g = g + jnp.dot(
                ms[rows, :], weights[patches : 2 * patches, columns], preferred_element_type=F32
            )
            trig_piece(tq, tj, tc, ts, tslot, (2 * h + 1) * quarter, quarter)
            halves.append(g)
        t_at = t_cols[pl.ds(sub_row(mq, mj), SUB), :]
        lo, hi = halves
        return (
            lo[:, : 2 * cases]
            + t_at[:, 0:1] * lo[:, 2 * cases :]
            + t_at[:, 1:2] * hi[:, : 2 * cases]
            + t_at[:, 2:3] * hi[:, 2 * cases :]
        )

    def a_copy(q, e):
        at = pl.multiple_of((q * (NY - 1) + e - 1) * SUB, SUB)
        return pltpu.make_async_remote_copy(
            src_ref=part_send.at[pl.ds(at, SUB)], dst_ref=part_recv.at[pl.ds(at, SUB)],
            send_sem=a_send.at[q * (NY - 1) + e - 1], recv_sem=a_recv.at[q * (NY - 1) + e - 1],
            device_id=at_y(e), device_id_type=MESH,
        )

    def b_copy(q, e):
        return pltpu.make_async_remote_copy(
            src_ref=row_send.at[pl.ds(pl.multiple_of(q * SUB + lax.rem(z + e, NZ) * OWN, OWN), OWN)],
            dst_ref=row_recv.at[pl.ds(pl.multiple_of((q * (NZ - 1) + e - 1) * OWN, OWN), OWN)],
            send_sem=b_send.at[q * (NZ - 1) + e - 1], recv_sem=b_recv.at[q * (NZ - 1) + e - 1],
            device_id=at_z(e), device_id_type=MESH,
        )

    def d_copy(q, e, came=False):
        source = lax.rem(z + NZ - e, NZ) if came else z
        rows = pl.ds(pl.multiple_of(q * ROWS + 3 * SUB + source * OWN, OWN), OWN)
        return pltpu.make_async_remote_copy(
            src_ref=res_all.at[rows], dst_ref=res_all.at[rows],
            send_sem=d_send.at[q * (NZ - 1) + e - 1], recv_sem=d_recv.at[q * (NZ - 1) + e - 1],
            device_id=at_z(e), device_id_type=MESH,
        )

    def e_copy(q, e):
        return pltpu.make_async_remote_copy(
            src_ref=res_all.at[pl.ds(pl.multiple_of(q * ROWS + 3 * SUB, SUB), SUB)],
            dst_ref=res_all.at[pl.ds(pl.multiple_of(q * ROWS + SLOT_OF_SEND[e] * SUB, SUB), SUB)],
            send_sem=e_send.at[q * (NY - 1) + e - 1], recv_sem=e_recv.at[q * (NY - 1) + e - 1],
            device_id=at_y(e), device_id_type=MESH,
        )

    def send_part(q, j, partial):
        e = DELTAS[j]
        at = pl.multiple_of((q * (NY - 1) + e - 1) * SUB, SUB)
        part_send[pl.ds(at, SUB), :] = partial.astype(BF)
        a_copy(q, e).start()

    def forward_tile(q):
        send_part(q, 0, forward_step(q, 1, 2 * q, q, 0, 2 * q))
        send_part(q, 1, forward_step(q, 2, 2 * q + 1, q, 1, 2 * q))
        send_part(q, 2, forward_step(q, 3, 2 * q + 1, q, 2, 2 * q + 1))
        after = lax.rem(q + 1, TILES)
        own = forward_step(after, 0, 2 * q + 2, q, 3, 2 * q + 1)
        part_own[pl.ds(pl.multiple_of(q * SUB, SUB), SUB), :] = own

    def sum_over_y(q):
        rows = pl.ds(pl.multiple_of(q * SUB, SUB), SUB)
        total = part_own[rows, :]
        for e in range(1, NY):
            a_copy(q, e).wait_recv()
        for e in range(1, NY):
            at = pl.multiple_of((q * (NY - 1) + e - 1) * SUB, SUB)
            total = total + part_recv[pl.ds(at, SUB), :].astype(F32)
        row_own[rows, :] = total
        row_send[rows, :] = total.astype(BF)
        for e in range(1, NZ):
            b_copy(q, e).start()

    def make_residual(q):
        total = row_own[pl.ds(pl.multiple_of(q * SUB + z * OWN, OWN), OWN), :]
        for e in range(1, NZ):
            b_copy(q, e).wait_recv()
        for e in range(1, NZ):
            at = pl.multiple_of((q * (NZ - 1) + e - 1) * OWN, OWN)
            total = total + row_recv[pl.ds(at, OWN), :].astype(F32)
        real, imag = -total[:, cases:], total[:, :cases]
        out_rows = pl.ds(pl.multiple_of(q * OWN, OWN), OWN)
        responses_ref[out_rows, :] = jnp.concatenate([real, imag], axis=1)
        magnitude = jnp.sqrt(real * real + imag * imag)
        weight = (magnitude - targets_ref[out_rows, :]) / jnp.maximum(magnitude, FLOOR)
        residual = jnp.concatenate([weight * real, weight * imag], axis=1).astype(BF)
        res_all[pl.ds(pl.multiple_of(q * ROWS + 3 * SUB + z * OWN, OWN), OWN), :] = residual
        for e in range(1, NZ):
            d_copy(q, e).start()

    def share_over_y(q):
        for e in range(1, NZ):
            d_copy(q, e, came=True).wait_recv()
        for e in range(1, NY):
            e_copy(q, e).start()

    def adjoint_tile(q):
        for e in range(1, NY):
            e_copy(q, e).wait_recv()
        for parity, (cos_ref, sin_ref) in enumerate(((cos_a, sin_a), (cos_b, sin_b))):
            pieces, t_pieces = [], []
            for j in (parity, parity + 2):
                at = pl.multiple_of(q * ROWS + j * SUB, SUB)
                pieces.append(res_all[pl.ds(at, SUB), :].astype(F32))
                t_pieces.append(t_rows[:, pl.ds(sub_row(q, j), SUB)])
            turned = jnp.concatenate(pieces, axis=0).T
            t_at = jnp.concatenate(t_pieces, axis=1)
            swapped = jnp.concatenate([turned[cases:], -turned[:cases]], axis=0)
            with_cos, with_sin = [swapped.astype(BF)], [turned.astype(BF)]
            for k in range(3):
                with_cos.append((swapped * t_at[k : k + 1, :]).astype(BF))
                with_sin.append((turned * t_at[k : k + 1, :]).astype(BF))
            rows = pl.ds(pl.multiple_of(q * 2 * SUB, 2 * SUB), 2 * SUB)
            acc[...] += jnp.dot(
                jnp.concatenate(with_cos, axis=0), cos_ref[rows, :], preferred_element_type=F32
            ) + jnp.dot(
                jnp.concatenate(with_sin, axis=0), sin_ref[rows, :], preferred_element_type=F32
            )

    for begin in range(0, SUB, quarter):
        trig_piece(0, 0, cos_a, sin_a, 0, begin, quarter)
    fetch.wait()
    pl.semaphore_wait(barrier, (NY - 1) + (NZ - 1) + len(group))

    def step(it, carry):
        pl.when(it < TILES)(lambda: forward_tile(it))
        pl.when(it >= 4)(lambda: adjoint_tile(it - 4))
        pl.when(jnp.logical_and(it >= 3, it < TILES + 3))(lambda: share_over_y(it - 3))
        pl.when(jnp.logical_and(it >= 2, it < TILES + 2))(lambda: make_residual(it - 2))
        pl.when(jnp.logical_and(it >= 1, it < TILES + 1))(lambda: sum_over_y(it - 1))
        return carry

    lax.fori_loop(0, TILES + 4, step, 0)

    half = 2 * cases

    def gradient(which):
        if which == 0:
            return acc[0:half, :] * scale_row
        total = acc[half : 2 * half, :] * face_rows[0:1, :]
        for k in range(1, 3):
            total = total + acc[(k + 1) * half : (k + 2) * half, :] * face_rows[k : k + 1, :]
        return total * scale_row

    for which in range(2):
        grad = gradient(which)

        @pl.when(core == which)
        def _():
            quarter_own[...] = grad

        @pl.when(core != which)
        def _():
            half_send[...] = grad.astype(BF)

    g_copy = pltpu.make_async_remote_copy(
        src_ref=half_send, dst_ref=half_recv, send_sem=g_send, recv_sem=g_recv,
        device_id=at_dir(0, 1), device_id_type=MESH,
    )
    g_copy.start()
    g_copy.wait()
    chip = quarter_own[...] + half_recv[...].astype(F32)
    quarter_own[...] = chip
    quarter_send[...] = chip.astype(BF)
    share = half // NX

    def h_copy(e):
        return pltpu.make_async_remote_copy(
            src_ref=quarter_send.at[pl.ds(pl.multiple_of(lax.rem(x + e, NX) * share, share), share)],
            dst_ref=quarter_recv.at[pl.ds((e - 1) * share, share)],
            send_sem=h_send.at[e - 1], recv_sem=h_recv.at[e - 1],
            device_id=at_dir(e, 0), device_id_type=MESH,
        )

    for e in range(1, NX):
        h_copy(e).start()
    total = quarter_own[pl.ds(pl.multiple_of(x * share, share), share), :]
    for e in range(1, NX):
        h_copy(e).wait()
    for e in range(1, NX):
        total = total + quarter_recv[(e - 1) * share : e * share, :].astype(F32)

    def place(ex, ec):
        at = lax.rem(core + ec, 2) * half + lax.rem(x + NX - ex, NX) * share
        return pl.ds(pl.multiple_of(at, share), share)

    grad_all[place(0, 0), :] = total.astype(BF)

    def k_copy(n, came=False):
        ex, ec = group[n]
        rows = place(ex, ec) if came else place(0, 0)
        return pltpu.make_async_remote_copy(
            src_ref=grad_all.at[rows], dst_ref=grad_all.at[rows],
            send_sem=k_send.at[n], recv_sem=k_recv.at[n],
            device_id=at_dir(ex, ec), device_id_type=MESH,
        )

    for n in range(len(group)):
        k_copy(n).start()
    for n in range(len(group)):
        k_copy(n, came=True).wait_recv()
    grad_v_ref[...] = grad_all[0:half, :].astype(F32).T
    grad_p_ref[...] = grad_all[half : 2 * half, :].astype(F32).T

    for n in range(len(group)):
        k_copy(n).wait_send()

    def drain(q, carry):
        for e in range(1, NY):
            a_copy(q, e).wait_send()
            e_copy(q, e).wait_send()
        for e in range(1, NZ):
            b_copy(q, e).wait_send()
            d_copy(q, e).wait_send()
        return carry

    lax.fori_loop(0, TILES, drain, 0)


def shards(direction_angles, positions, normal_angles, areas, pressure, velocity, targets):
    cases = targets.shape[1]
    patches = positions.shape[1]
    dirs = direction_angles.shape[1]
    total_patches = patches * lax.axis_size("surf")
    owners = NY * NZ
    angles = direction_angles.reshape(2, owners, TILES, OWN).transpose(0, 2, 1, 3).reshape(2, dirs)
    vmem = pl.BlockSpec(memory_space=pltpu.VMEM)
    half = 2 * cases
    dma = pltpu.SemaphoreType.DMA
    slots = 2 * TILES + 1
    return pl.pallas_call(
        functools.partial(body, total_patches),
        out_shape=(
            jax.ShapeDtypeStruct((dirs // owners, half), F32),
            jax.ShapeDtypeStruct((patches, half), F32),
            jax.ShapeDtypeStruct((patches, half), F32),
        ),
        in_specs=[vmem] * 6 + [pl.BlockSpec(memory_space=pl.ANY)],
        out_specs=(vmem, vmem, vmem),
        scratch_shapes=[
            pltpu.VMEM((TILES * OWN, cases), F32),
            pltpu.VMEM((32, dirs), F32),
            pltpu.VMEM((32, patches), F32),
            pltpu.VMEM((8, dirs), F32),
            pltpu.VMEM((dirs, 8), F32),
            pltpu.VMEM((dirs, 32), BF),
            pltpu.VMEM((32, patches), BF),
            pltpu.VMEM((8, patches), F32),
            pltpu.VMEM((2 * patches, 4 * half), BF),
            pltpu.VMEM((slots * SUB, patches), BF),
            pltpu.VMEM((slots * SUB, patches), BF),
            pltpu.VMEM((slots * SUB, patches), BF),
            pltpu.VMEM((slots * SUB, patches), BF),
            pltpu.VMEM((TILES * (NY - 1) * SUB, half), BF),
            pltpu.VMEM((TILES * SUB, half), F32),
            pltpu.VMEM((TILES * (NY - 1) * SUB, half), BF),
            pltpu.VMEM((TILES * SUB, half), F32),
            pltpu.VMEM((TILES * SUB, half), BF),
            pltpu.VMEM((TILES * (NZ - 1) * OWN, half), BF),
            pltpu.VMEM((TILES * ROWS, half), BF),
            pltpu.VMEM((4 * half, patches), F32),
            pltpu.VMEM((half, patches), BF),
            pltpu.VMEM((half, patches), BF),
            pltpu.VMEM((half, patches), F32),
            pltpu.VMEM((half, patches), BF),
            pltpu.VMEM((half // NX * (NX - 1), patches), BF),
            pltpu.VMEM((2 * half, patches), BF),
            dma,
            dma((TILES * (NY - 1),)), dma((TILES * (NY - 1),)),
            dma((TILES * (NZ - 1),)), dma((TILES * (NZ - 1),)),
            dma((TILES * (NZ - 1),)), dma((TILES * (NZ - 1),)),
            dma((TILES * (NY - 1),)), dma((TILES * (NY - 1),)),
            dma, dma,
            dma((NX - 1,)), dma((NX - 1,)),
            dma((2 * NX - 1,)), dma((2 * NX - 1,)),
        ],
        compiler_params=pltpu.CompilerParams(
            collective_id=0, has_side_effects=True, vmem_limit_bytes=56 * 2**20
        ),
    )(
        angles, positions, normal_angles, areas.reshape(1, patches), pressure, velocity, targets
    )


def solution(mesh):
    in_specs = (
        P(None, "dir"),
        P(None, "surf"),
        P(None, "surf"),
        P("surf"),
        P("surf", None),
        P("surf", None),
        P("dir", None),
    )
    out_specs = (P(("dir", "surf"), None), P("surf", None), P("surf", None))
    return jax.shard_map(shards, mesh=mesh, in_specs=in_specs, out_specs=out_specs, check_vma=False)
```

```python
import functools
import math

import jax
import jax.numpy as jnp
from jax import lax
from jax.experimental import pallas as pl
from jax.experimental.pallas import tpu as pltpu
from jax.sharding import PartitionSpec as P

MESH = pl.DeviceIdType.MESH
BF = jnp.bfloat16
F32 = jnp.float32
FLOOR = 0.5

TILES = 4
NY, NZ, NX = 4, 8, 4
OWN = 32
SUB = NZ * OWN
ROWS = NY * SUB
DELTAS = (2, 1, 3, 0)
OURS = 3
SLOT_OF_SEND = {1: 2, 2: 0, 3: 1}

ROOT2 = math.sqrt(2.0)
SIN_HALF = [c * ROOT2 for c in (3.14158198, -5.1671413, 2.54188707, -0.55460885)]
COS_HALF = [c * ROOT2 for c in (0.99999325, -4.93393467, 4.0412481, -1.22203176)]
SIN_FINE = [c * ROOT2 for c in (3.14159258, -5.16770687, 2.55003119, -0.59804419, 0.07721839)]
COS_FINE = [c * ROOT2 for c in (0.99999995, -4.93479283, 4.05841135, -1.33187657, 0.21968961)]


def horner(coefficients, square):
    value = coefficients[-1]
    for coefficient in coefficients[-2::-1]:
        value = value * square + coefficient
    return value


def cos_sin(cycles, sin_half, cos_half):
    rest = cycles - jnp.round(cycles)
    square = rest * rest
    half_sine = horner(sin_half, square) * rest
    half_cosine = horner(cos_half, square)
    return 1.0 - half_sine * half_sine, half_sine * half_cosine


def fine_cos_sin(angle):
    return cos_sin(angle * F32(1.0 / (2.0 * math.pi)), SIN_FINE, COS_FINE)


def unit_rows(angles):
    cos_all, sin_all = fine_cos_sin(angles)
    cos_polar, sin_polar = cos_all[0:1], sin_all[0:1]
    cos_azimuth, sin_azimuth = cos_all[1:2], sin_all[1:2]
    return sin_polar * cos_azimuth, sin_polar * sin_azimuth, cos_polar


def three_parts(value):
    first = value.astype(BF).astype(F32)
    second = (value - first).astype(BF).astype(F32)
    return first, second, value - first - second


def body(
    total_patches,
    angles_ref, positions_ref, normals_ref, areas_ref, pressure_ref, velocity_ref, targets_hbm,
    responses_ref, grads_ref,
    targets_t, targets_ref, angle_rows, angle_cols, angle_perm, split_t, split_x, t_rows, t_cols, t_lhs, x_rhs, face_rows, weights,
    cos_a, sin_a, cos_b, sin_b,
    part_send, part_recv, part_own, row_own, row_send, row_recv, res_all, acc,
    half_send, half_recv, quarter_own, quarter_send, quarter_recv, grad_all,
    local_sem, a_send, a_recv, b_send, b_recv, d_send, d_recv,
    e_send, e_recv,
    g_send, g_recv, h_send, h_recv, k_send, k_recv, m_send, m_recv,
):
    dir_index = lax.axis_index("dir")
    surf_index = lax.axis_index("surf")
    x, core = dir_index // 2, lax.rem(dir_index, 2)
    y, z = surf_index // NZ, lax.rem(surf_index, NZ)
    patches = positions_ref.shape[1]

    def at_y(e):
        return (dir_index, lax.rem(y + e, NY) * NZ + z)

    def at_z(e):
        return (dir_index, y * NZ + lax.rem(z + e, NZ))

    def at_dir(ex, ec):
        return (lax.rem(x + ex, NX) * 2 + lax.rem(core + ec, 2), surf_index)

    group = [(ex, 0) for ex in range(1, NX)] + [(0, 1)]
    barrier = pltpu.get_barrier_semaphore()
    for e in range(1, NY):
        pl.semaphore_signal(barrier, inc=1, device_id=at_y(e), device_id_type=MESH)
    for e in range(1, NZ):
        pl.semaphore_signal(barrier, inc=1, device_id=at_z(e), device_id_type=MESH)
    for ex, ec in group:
        pl.semaphore_signal(barrier, inc=1, device_id=at_dir(ex, ec), device_id_type=MESH)

    own_rows = TILES * OWN
    fetch = pltpu.make_async_copy(
        targets_hbm.at[:, pl.ds(pl.multiple_of(surf_index * own_rows, own_rows), own_rows)],
        targets_t, local_sem,
    )
    fetch.start()

    angle_rows[...] = jnp.zeros_like(angle_rows)
    angle_rows[0:2, :] = angles_ref[...]
    angle_cols[...] = angle_rows[...].T
    for q in range(TILES):
        for owner in range(NY * NZ):
            begin, source = q * ROWS + owner * OWN, owner * own_rows + q * OWN
            angle_perm[begin : begin + OWN, :] = angle_cols[source : source + OWN, :]
    tx, ty, tz = unit_rows(angle_perm[...].T)
    split_t[...] = jnp.zeros_like(split_t)
    split_x[...] = jnp.zeros_like(split_x)
    t_rows[...] = jnp.zeros_like(t_rows)
    for k, row in enumerate((tx, ty, tz)):
        t_rows[k : k + 1, :] = row
        first, second, third = three_parts(row)
        for at, part in enumerate((first, first, second, second, first, third)):
            split_t[3 * at + k : 3 * at + k + 1, :] = part
        first, second, third = three_parts(positions_ref[k : k + 1, :] * F32(0.5 / math.pi))
        for at, part in enumerate((first, second, first, second, third, first)):
            split_x[3 * at + k : 3 * at + k + 1, :] = part
    x_rhs[...] = split_x[...].astype(BF)
    t_lhs[...] = split_t[...].T.astype(BF)
    t_cols[...] = t_rows[...].T

    face_rows[...] = jnp.zeros_like(face_rows)
    for at in range(areas_ref.shape[0]):
        face_rows[3:4, 128 * at : 128 * (at + 1)] = areas_ref[at : at + 1, :]
    scale_row = face_rows[3:4, :] * F32(1.0 / math.sqrt(total_patches))
    for k, row in enumerate(unit_rows(normals_ref[...])):
        face_rows[k : k + 1, :] = row
    face_rows[3:4, :] = scale_row
    face_cols = face_rows[...].T
    scale_col = face_cols[:, 3:4]
    weighted_p = (pressure_ref[...].astype(F32) * scale_col).astype(BF).astype(F32)
    weighted_v = (velocity_ref[...].astype(F32) * scale_col).astype(BF).astype(F32)
    cases = weighted_p.shape[1] // 2
    for k in range(4):
        source = weighted_v if k == 0 else weighted_p * face_cols[:, k - 1 : k]
        turned = jnp.concatenate([source[:, cases:], -source[:, :cases]], axis=1)
        columns = slice(k * 2 * cases, (k + 1) * 2 * cases)
        weights[0:patches, columns] = source.astype(BF)
        weights[patches : 2 * patches, columns] = turned.astype(BF)
    acc[...] = jnp.zeros_like(acc)

    def sub_row(q, j):
        return pl.multiple_of(q * ROWS + lax.rem(y + DELTAS[j], NY) * SUB, SUB)

    def trig_piece(q, j, cos_ref, sin_ref, slot, begin, count):
        angle = jnp.dot(
            t_lhs[pl.ds(sub_row(q, j) + begin, count), :], x_rhs[...], preferred_element_type=F32
        )
        cosine, sine = cos_sin(angle, SIN_HALF, COS_HALF)
        at = pl.multiple_of(slot * SUB + begin, count)
        cos_ref[pl.ds(at, count), :] = cosine.astype(BF)
        sin_ref[pl.ds(at, count), :] = sine.astype(BF)

    quarter = SUB // 4

    def forward_step(q, j, after=None):
        def make(piece):
            if after is not None:
                tq, tj, slot = after
                tc, ts = (cos_a, sin_a) if tj % 2 == 0 else (cos_b, sin_b)
                trig_piece(tq, tj, tc, ts, slot, piece * quarter, quarter)

        mc, ms = (cos_a, sin_a) if j % 2 == 0 else (cos_b, sin_b)
        rows = pl.ds(pl.multiple_of((2 * q + j // 2) * SUB, SUB), SUB)
        halves = []
        for h in range(2):
            columns = slice(4 * cases * h, 4 * cases * (h + 1))
            g = jnp.dot(mc[rows, :], weights[0:patches, columns], preferred_element_type=F32)
            make(2 * h)
            g = g + jnp.dot(
                ms[rows, :], weights[patches : 2 * patches, columns], preferred_element_type=F32
            )
            make(2 * h + 1)
            halves.append(g)
        t_at = t_cols[pl.ds(sub_row(q, j), SUB), :]
        lo, hi = halves
        return (
            lo[:, : 2 * cases]
            + t_at[:, 0:1] * lo[:, 2 * cases :]
            + t_at[:, 1:2] * hi[:, : 2 * cases]
            + t_at[:, 2:3] * hi[:, 2 * cases :]
        )

    def a_rows(q, e):
        return pl.ds(pl.multiple_of((q * (NY - 1) + e - 1) * SUB, SUB), SUB)

    def a_copy(q, e):
        return pltpu.make_async_remote_copy(
            src_ref=part_send.at[a_rows(q, e)], dst_ref=part_recv.at[a_rows(q, e)],
            send_sem=a_send.at[q * (NY - 1) + e - 1], recv_sem=a_recv.at[q * (NY - 1) + e - 1],
            device_id=at_y(e), device_id_type=MESH,
        )

    def b_copy(q, e):
        return pltpu.make_async_remote_copy(
            src_ref=row_send.at[pl.ds(pl.multiple_of(q * SUB + lax.rem(z + e, NZ) * OWN, OWN), OWN)],
            dst_ref=row_recv.at[pl.ds(pl.multiple_of((q * (NZ - 1) + e - 1) * OWN, OWN), OWN)],
            send_sem=b_send.at[q * (NZ - 1) + e - 1], recv_sem=b_recv.at[q * (NZ - 1) + e - 1],
            device_id=at_z(e), device_id_type=MESH,
        )

    def d_copy(q, e, came=False):
        source = lax.rem(z + NZ - e, NZ) if came else z
        rows = pl.ds(pl.multiple_of(q * ROWS + OURS * SUB + source * OWN, OWN), OWN)
        return pltpu.make_async_remote_copy(
            src_ref=res_all.at[rows], dst_ref=res_all.at[rows],
            send_sem=d_send.at[q * (NZ - 1) + e - 1], recv_sem=d_recv.at[q * (NZ - 1) + e - 1],
            device_id=at_z(e), device_id_type=MESH,
        )

    def e_copy(q, e):
        return pltpu.make_async_remote_copy(
            src_ref=res_all.at[pl.ds(pl.multiple_of(q * ROWS + OURS * SUB, SUB), SUB)],
            dst_ref=res_all.at[pl.ds(pl.multiple_of(q * ROWS + SLOT_OF_SEND[e] * SUB, SUB), SUB)],
            send_sem=e_send.at[q * (NY - 1) + e - 1], recv_sem=e_recv.at[q * (NY - 1) + e - 1],
            device_id=at_y(e), device_id_type=MESH,
        )

    def step_0(q):
        part_send[a_rows(q, DELTAS[0]), :] = forward_step(q, 0, (q, 1, 2 * q)).astype(BF)

    def step_1(q):
        part_send[a_rows(q, DELTAS[1]), :] = forward_step(q, 1, (q, 2, 2 * q + 1)).astype(BF)

        @pl.when(q == 0)
        def _():
            pl.semaphore_wait(barrier, (NY - 1) + (NZ - 1) + len(group))

        a_copy(q, DELTAS[0]).start()
        a_copy(q, DELTAS[1]).start()

    def step_2(q):
        part_send[a_rows(q, DELTAS[2]), :] = forward_step(q, 2, (q, 3, 2 * q + 1)).astype(BF)
        a_copy(q, DELTAS[2]).start()

    def step_3(q):
        rows = pl.ds(pl.multiple_of(q * SUB, SUB), SUB)

        @pl.when(q < TILES - 1)
        def _():
            part_own[rows, :] = forward_step(q, 3, (q + 1, 0, 2 * q + 2))

        @pl.when(q == TILES - 1)
        def _():
            part_own[rows, :] = forward_step(q, 3)

    def sum_over_y(q):
        rows = pl.ds(pl.multiple_of(q * SUB, SUB), SUB)
        total = part_own[rows, :]
        for e in range(1, NY):
            a_copy(q, e).wait_recv()
        for e in range(1, NY):
            total = total + part_recv[a_rows(q, e), :].astype(F32)
        row_own[rows, :] = total
        row_send[rows, :] = total.astype(BF)
        for e in range(1, NZ):
            b_copy(q, e).start()

    def make_residual(q):
        total = row_own[pl.ds(pl.multiple_of(q * SUB + z * OWN, OWN), OWN), :]
        for e in range(1, NZ):
            b_copy(q, e).wait_recv()
        for e in range(1, NZ):
            at = pl.multiple_of((q * (NZ - 1) + e - 1) * OWN, OWN)
            total = total + row_recv[pl.ds(at, OWN), :].astype(F32)
        real, imag = -total[:, cases:], total[:, :cases]
        out_rows = pl.ds(pl.multiple_of(q * OWN, OWN), OWN)
        responses_ref[out_rows, :] = jnp.concatenate([real, imag], axis=1)
        magnitude = jnp.sqrt(real * real + imag * imag)
        weight = (magnitude - targets_ref[out_rows, :]) / jnp.maximum(magnitude, FLOOR)
        residual = jnp.concatenate([weight * real, weight * imag], axis=1).astype(BF)
        res_all[pl.ds(pl.multiple_of(q * ROWS + OURS * SUB + z * OWN, OWN), OWN), :] = residual
        for e in range(1, NZ):
            d_copy(q, e).start()

    def share_over_y(q):
        for e in range(1, NZ):
            d_copy(q, e, came=True).wait_recv()
        for e in range(1, NY):
            e_copy(q, e).start()

    def adjoint_tile(q):
        for e in range(1, NY):
            e_copy(q, e).wait_recv()
        for parity, cos_ref, sin_ref in ((1, cos_b, sin_b), (0, cos_a, sin_a)):
            pieces, t_pieces = [], []
            for j in (parity, parity + 2):
                at = pl.multiple_of(q * ROWS + j * SUB, SUB)
                pieces.append(res_all[pl.ds(at, SUB), :].astype(F32))
                t_pieces.append(t_rows[:, pl.ds(sub_row(q, j), SUB)])
            turned = jnp.concatenate(pieces, axis=0).T
            t_at = jnp.concatenate(t_pieces, axis=1)
            swapped = jnp.concatenate([turned[cases:], -turned[:cases]], axis=0)
            with_cos, with_sin = [swapped.astype(BF)], [turned.astype(BF)]
            for k in range(3):
                with_cos.append((swapped * t_at[k : k + 1, :]).astype(BF))
                with_sin.append((turned * t_at[k : k + 1, :]).astype(BF))
            rows = pl.ds(pl.multiple_of(q * 2 * SUB, 2 * SUB), 2 * SUB)
            acc[...] += jnp.dot(
                jnp.concatenate(with_cos, axis=0), cos_ref[rows, :], preferred_element_type=F32
            ) + jnp.dot(
                jnp.concatenate(with_sin, axis=0), sin_ref[rows, :], preferred_element_type=F32
            )

    for begin in range(0, SUB, quarter):
        trig_piece(0, 0, cos_a, sin_a, 0, begin, quarter)
    fetch.wait()
    targets_ref[...] = targets_t[...].T

    def step(it, carry):
        def when(work, lag):
            inside = jnp.logical_and(it >= lag, it < TILES + lag)
            pl.when(inside)(lambda: work(it - lag))

        when(step_0, 0)
        when(step_1, 0)
        when(make_residual, 3)
        when(step_2, 0)
        when(step_3, 0)
        when(share_over_y, 4)
        when(sum_over_y, 1)
        when(adjoint_tile, 6)
        return carry

    lax.fori_loop(0, TILES + 6, step, 0)

    half = 2 * cases

    def gradient(which):
        if which == 0:
            return acc[0:half, :] * scale_row
        total = acc[half : 2 * half, :] * face_rows[0:1, :]
        for k in range(1, 3):
            total = total + acc[(k + 1) * half : (k + 2) * half, :] * face_rows[k : k + 1, :]
        return total * scale_row

    for which in range(2):
        grad = gradient(which)

        @pl.when(core == which)
        def _():
            quarter_own[...] = grad

        @pl.when(core != which)
        def _():
            half_send[...] = grad.astype(BF)

    g_copy = pltpu.make_async_remote_copy(
        src_ref=half_send, dst_ref=half_recv, send_sem=g_send, recv_sem=g_recv,
        device_id=at_dir(0, 1), device_id_type=MESH,
    )
    g_copy.start()
    g_copy.wait()
    chip = quarter_own[...] + half_recv[...].astype(F32)
    quarter_own[...] = chip
    quarter_send[...] = chip.astype(BF)
    share = half // NX

    def h_copy(e):
        return pltpu.make_async_remote_copy(
            src_ref=quarter_send.at[pl.ds(pl.multiple_of(lax.rem(x + e, NX) * share, share), share)],
            dst_ref=quarter_recv.at[pl.ds((e - 1) * share, share)],
            send_sem=h_send.at[e - 1], recv_sem=h_recv.at[e - 1],
            device_id=at_dir(e, 0), device_id_type=MESH,
        )

    for e in range(1, NX):
        h_copy(e).start()
    total = quarter_own[pl.ds(pl.multiple_of(x * share, share), share), :]
    for e in range(1, NX):
        h_copy(e).wait()
    for e in range(1, NX):
        total = total + quarter_recv[(e - 1) * share : e * share, :].astype(F32)

    def place(ex, ec):
        at = lax.rem(core + ec, 2) * half + lax.rem(x + NX - ex, NX) * share
        return pl.ds(pl.multiple_of(at, share), share)

    grad_all[place(0, 0), :] = total.astype(BF)

    def k_copy(e, came=False):
        rows = place(e, 0) if came else place(0, 0)
        return pltpu.make_async_remote_copy(
            src_ref=grad_all.at[rows], dst_ref=grad_all.at[rows],
            send_sem=k_send.at[e - 1], recv_sem=k_recv.at[e - 1],
            device_id=at_dir(e, 0), device_id_type=MESH,
        )

    def m_copy(e, came=False):
        rows = place(e, 1) if came else place(e, 0)
        return pltpu.make_async_remote_copy(
            src_ref=grad_all.at[rows], dst_ref=grad_all.at[rows],
            send_sem=m_send.at[e], recv_sem=m_recv.at[e],
            device_id=at_dir(0, 1), device_id_type=MESH,
        )

    for e in range(1, NX):
        k_copy(e).start()
    m_copy(0).start()
    for e in (1, 3, 2):
        k_copy(e, came=True).wait_recv()
        m_copy(e).start()
    for e in range(NX):
        m_copy(e, came=True).wait_recv()
    grads_ref[...] = grad_all[...]

    for e in range(1, NX):
        k_copy(e).wait_send()
    for e in range(NX):
        m_copy(e).wait_send()

    def drain(q, carry):
        for e in range(1, NY):
            a_copy(q, e).wait_send()
            e_copy(q, e).wait_send()
        for e in range(1, NZ):
            b_copy(q, e).wait_send()
            d_copy(q, e).wait_send()
        return carry

    lax.fori_loop(0, TILES, drain, 0)


def finish(responses_ref, grads_ref, out_ref, grad_p_ref, grad_v_ref):
    half = grads_ref.shape[0] // 2
    out_ref[...] = responses_ref[...]
    grad_v_ref[...] = grads_ref[0:half, :].astype(F32).T
    grad_p_ref[...] = grads_ref[half : 2 * half, :].astype(F32).T


def shards(direction_angles, positions, normal_angles, areas, pressure, velocity, targets):
    cases = targets.shape[1]
    patches = positions.shape[1]
    dirs = direction_angles.shape[1]
    total_patches = patches * lax.axis_size("surf")
    owners = NY * NZ
    vmem = pl.BlockSpec(memory_space=pltpu.VMEM)
    half = 2 * cases
    dma = pltpu.SemaphoreType.DMA
    slots = 2 * TILES
    responses, grads = pl.pallas_call(
        functools.partial(body, total_patches),
        out_shape=(
            jax.ShapeDtypeStruct((dirs // owners, half), F32),
            jax.ShapeDtypeStruct((2 * half, patches), BF),
        ),
        in_specs=[vmem] * 6 + [pl.BlockSpec(memory_space=pl.ANY)],
        out_specs=(vmem, vmem),
        scratch_shapes=[
            pltpu.VMEM((cases, TILES * OWN), F32),
            pltpu.VMEM((TILES * OWN, cases), F32),
            pltpu.VMEM((8, dirs), F32),
            pltpu.VMEM((dirs, 8), F32),
            pltpu.VMEM((dirs, 8), F32),
            pltpu.VMEM((32, dirs), F32),
            pltpu.VMEM((32, patches), F32),
            pltpu.VMEM((8, dirs), F32),
            pltpu.VMEM((dirs, 8), F32),
            pltpu.VMEM((dirs, 32), BF),
            pltpu.VMEM((32, patches), BF),
            pltpu.VMEM((8, patches), F32),
            pltpu.VMEM((2 * patches, 4 * half), BF),
            pltpu.VMEM((slots * SUB, patches), BF),
            pltpu.VMEM((slots * SUB, patches), BF),
            pltpu.VMEM((slots * SUB, patches), BF),
            pltpu.VMEM((slots * SUB, patches), BF),
            pltpu.VMEM((TILES * (NY - 1) * SUB, half), BF),
            pltpu.VMEM((TILES * (NY - 1) * SUB, half), BF),
            pltpu.VMEM((TILES * SUB, half), F32),
            pltpu.VMEM((TILES * SUB, half), F32),
            pltpu.VMEM((TILES * SUB, half), BF),
            pltpu.VMEM((TILES * (NZ - 1) * OWN, half), BF),
            pltpu.VMEM((TILES * ROWS, half), BF),
            pltpu.VMEM((4 * half, patches), F32),
            pltpu.VMEM((half, patches), BF),
            pltpu.VMEM((half, patches), BF),
            pltpu.VMEM((half, patches), F32),
            pltpu.VMEM((half, patches), BF),
            pltpu.VMEM((half // NX * (NX - 1), patches), BF),
            pltpu.VMEM((2 * half, patches), BF),
            dma,
            dma((TILES * (NY - 1),)), dma((TILES * (NY - 1),)),
            dma((TILES * (NZ - 1),)), dma((TILES * (NZ - 1),)),
            dma((TILES * (NZ - 1),)), dma((TILES * (NZ - 1),)),
            dma((TILES * (NY - 1),)), dma((TILES * (NY - 1),)),
            dma, dma,
            dma((NX - 1,)), dma((NX - 1,)),
            dma((NX - 1,)), dma((NX - 1,)),
            dma((NX,)), dma((NX,)),
        ],
        compiler_params=pltpu.CompilerParams(
            collective_id=0, has_side_effects=True, vmem_limit_bytes=56 * 2**20
        ),
    )(
        direction_angles, positions, normal_angles, areas.reshape(patches // 128, 128),
        pressure, velocity, targets.T,
    )
    return pl.pallas_call(
        finish,
        out_shape=(
            jax.ShapeDtypeStruct((dirs // owners, half), F32),
            jax.ShapeDtypeStruct((patches, half), F32),
            jax.ShapeDtypeStruct((patches, half), F32),
        ),
        in_specs=[vmem] * 2,
        out_specs=(vmem, vmem, vmem),
    )(responses, grads)


def solution(mesh):
    in_specs = (
        P(None, "dir"),
        P(None, "surf"),
        P(None, "surf"),
        P("surf"),
        P("surf", None),
        P("surf", None),
        P("dir", None),
    )
    out_specs = (P(("dir", "surf"), None), P("surf", None), P("surf", None))
    return jax.shard_map(shards, mesh=mesh, in_specs=in_specs, out_specs=out_specs, check_vma=False)
```

```python
import functools
import math

import jax
import jax.numpy as jnp
from jax import lax
from jax.experimental import pallas as pl
from jax.experimental.pallas import tpu as pltpu
from jax.sharding import PartitionSpec as P

MESH = pl.DeviceIdType.MESH
BF = jnp.bfloat16
F32 = jnp.float32
FLOOR = 0.5

TILES = 4
NY, NZ, NX = 4, 8, 4
OWN = 32
SUB = NZ * OWN
ROWS = NY * SUB
DELTAS = (2, 1, 3, 0)
OURS = 3
SLOT_OF_SEND = {1: 2, 2: 0, 3: 1}

ROOT2 = math.sqrt(2.0)
SIN_HALF = [c * ROOT2 for c in (3.14158198, -5.1671413, 2.54188707, -0.55460885)]
SIN_FINE = [c * ROOT2 for c in (3.14159258, -5.16770687, 2.55003119, -0.59804419, 0.07721839)]
COS_FINE = [c * ROOT2 for c in (0.99999995, -4.93479283, 4.05841135, -1.33187657, 0.21968961)]


def horner(coefficients, square):
    value = coefficients[-1]
    for coefficient in coefficients[-2::-1]:
        value = value * square + coefficient
    return value


def cos_sin(cycles):
    rest = cycles - jnp.round(cycles)
    half_sine = horner(SIN_HALF, rest * rest) * rest
    double = half_sine * half_sine
    left = jnp.maximum(2.0 - double, 1e-20)
    return 1.0 - double, half_sine * (left * lax.rsqrt(left))


def fine_cos_sin(angle):
    cycles = angle * F32(1.0 / (2.0 * math.pi))
    rest = cycles - jnp.round(cycles)
    square = rest * rest
    half_sine = horner(SIN_FINE, square) * rest
    return 1.0 - half_sine * half_sine, half_sine * horner(COS_FINE, square)


def unit_rows(angles):
    cos_all, sin_all = fine_cos_sin(angles)
    cos_polar, sin_polar = cos_all[0:1], sin_all[0:1]
    cos_azimuth, sin_azimuth = cos_all[1:2], sin_all[1:2]
    return sin_polar * cos_azimuth, sin_polar * sin_azimuth, cos_polar


def three_parts(value):
    first = value.astype(BF).astype(F32)
    second = (value - first).astype(BF).astype(F32)
    return first, second, value - first - second


def body(
    total_patches,
    angles_ref, positions_ref, normals_ref, areas_ref, pressure_ref, velocity_ref, targets_hbm,
    responses_ref, grads_ref,
    targets_t, targets_ref, angle_rows, angle_cols, angle_perm, split_t, split_x, t_rows, t_cols, t_lhs, x_rhs, face_rows, weights,
    cos_a, sin_a, cos_b, sin_b,
    part_send, part_recv, part_own, row_own, row_send, row_recv, res_all, acc,
    half_send, half_recv, quarter_own, quarter_send, quarter_recv, grad_all,
    local_sem, a_send, a_recv, b_send, b_recv, d_send, d_recv,
    e_send, e_recv,
    g_send, g_recv, h_send, h_recv, k_send, k_recv, m_send, m_recv,
):
    dir_index = lax.axis_index("dir")
    surf_index = lax.axis_index("surf")
    x, core = dir_index // 2, lax.rem(dir_index, 2)
    y, z = surf_index // NZ, lax.rem(surf_index, NZ)
    patches = positions_ref.shape[1]

    def at_y(e):
        return (dir_index, lax.rem(y + e, NY) * NZ + z)

    def at_z(e):
        return (dir_index, y * NZ + lax.rem(z + e, NZ))

    def at_dir(ex, ec):
        return (lax.rem(x + ex, NX) * 2 + lax.rem(core + ec, 2), surf_index)

    group = [(ex, 0) for ex in range(1, NX)] + [(0, 1)]
    barrier = pltpu.get_barrier_semaphore()
    for e in range(1, NY):
        pl.semaphore_signal(barrier, inc=1, device_id=at_y(e), device_id_type=MESH)
    for e in range(1, NZ):
        pl.semaphore_signal(barrier, inc=1, device_id=at_z(e), device_id_type=MESH)
    for ex, ec in group:
        pl.semaphore_signal(barrier, inc=1, device_id=at_dir(ex, ec), device_id_type=MESH)

    own_rows = TILES * OWN
    fetch = pltpu.make_async_copy(
        targets_hbm.at[:, pl.ds(pl.multiple_of(surf_index * own_rows, own_rows), own_rows)],
        targets_t, local_sem,
    )
    fetch.start()

    angle_rows[...] = jnp.zeros_like(angle_rows)
    angle_rows[0:2, :] = angles_ref[...]
    angle_cols[...] = angle_rows[...].T
    for q in range(TILES):
        for owner in range(NY * NZ):
            begin, source = q * ROWS + owner * OWN, owner * own_rows + q * OWN
            angle_perm[begin : begin + OWN, :] = angle_cols[source : source + OWN, :]
    tx, ty, tz = unit_rows(angle_perm[...].T)
    split_t[...] = jnp.zeros_like(split_t)
    split_x[...] = jnp.zeros_like(split_x)
    t_rows[...] = jnp.zeros_like(t_rows)
    for k, row in enumerate((tx, ty, tz)):
        t_rows[k : k + 1, :] = row
        first, second, third = three_parts(row)
        for at, part in enumerate((first, first, second, second, first, third)):
            split_t[3 * at + k : 3 * at + k + 1, :] = part
        first, second, third = three_parts(positions_ref[k : k + 1, :] * F32(0.5 / math.pi))
        for at, part in enumerate((first, second, first, second, third, first)):
            split_x[3 * at + k : 3 * at + k + 1, :] = part
    x_rhs[...] = split_x[...].astype(BF)
    t_lhs[...] = split_t[...].T.astype(BF)
    t_cols[...] = t_rows[...].T

    face_rows[...] = jnp.zeros_like(face_rows)
    for at in range(areas_ref.shape[0]):
        face_rows[3:4, 128 * at : 128 * (at + 1)] = areas_ref[at : at + 1, :]
    scale_row = face_rows[3:4, :] * F32(1.0 / math.sqrt(total_patches))
    for k, row in enumerate(unit_rows(normals_ref[...])):
        face_rows[k : k + 1, :] = row
    face_rows[3:4, :] = scale_row
    face_cols = face_rows[...].T
    scale_col = face_cols[:, 3:4]
    weighted_p = (pressure_ref[...].astype(F32) * scale_col).astype(BF).astype(F32)
    weighted_v = (velocity_ref[...].astype(F32) * scale_col).astype(BF).astype(F32)
    cases = weighted_p.shape[1] // 2
    for k in range(4):
        source = weighted_v if k == 0 else weighted_p * face_cols[:, k - 1 : k]
        turned = jnp.concatenate([source[:, cases:], -source[:, :cases]], axis=1)
        columns = slice(k * 2 * cases, (k + 1) * 2 * cases)
        weights[0:patches, columns] = source.astype(BF)
        weights[patches : 2 * patches, columns] = turned.astype(BF)
    acc[...] = jnp.zeros_like(acc)

    def sub_row(q, j):
        return pl.multiple_of(q * ROWS + lax.rem(y + DELTAS[j], NY) * SUB, SUB)

    def trig_piece(q, j, cos_ref, sin_ref, slot, begin, count):
        angle = jnp.dot(
            t_lhs[pl.ds(sub_row(q, j) + begin, count), :], x_rhs[...], preferred_element_type=F32
        )
        cosine, sine = cos_sin(angle)
        at = pl.multiple_of(slot * SUB + begin, count)
        cos_ref[pl.ds(at, count), :] = cosine.astype(BF)
        sin_ref[pl.ds(at, count), :] = sine.astype(BF)

    quarter = SUB // 4

    def forward_step(q, j, after=None):
        def make(piece):
            if after is not None:
                tq, tj, slot = after
                tc, ts = (cos_a, sin_a) if tj % 2 == 0 else (cos_b, sin_b)
                trig_piece(tq, tj, tc, ts, slot, piece * quarter, quarter)

        mc, ms = (cos_a, sin_a) if j % 2 == 0 else (cos_b, sin_b)
        rows = pl.ds(pl.multiple_of((2 * q + j // 2) * SUB, SUB), SUB)
        halves = []
        for h in range(2):
            columns = slice(4 * cases * h, 4 * cases * (h + 1))
            g = jnp.dot(mc[rows, :], weights[0:patches, columns], preferred_element_type=F32)
            make(2 * h)
            g = g + jnp.dot(
                ms[rows, :], weights[patches : 2 * patches, columns], preferred_element_type=F32
            )
            make(2 * h + 1)
            halves.append(g)
        t_at = t_cols[pl.ds(sub_row(q, j), SUB), :]
        lo, hi = halves
        return (
            lo[:, : 2 * cases]
            + t_at[:, 0:1] * lo[:, 2 * cases :]
            + t_at[:, 1:2] * hi[:, : 2 * cases]
            + t_at[:, 2:3] * hi[:, 2 * cases :]
        )

    def a_rows(q, e):
        return pl.ds(pl.multiple_of((q * (NY - 1) + e - 1) * SUB, SUB), SUB)

    def a_copy(q, e):
        return pltpu.make_async_remote_copy(
            src_ref=part_send.at[a_rows(q, e)], dst_ref=part_recv.at[a_rows(q, e)],
            send_sem=a_send.at[q * (NY - 1) + e - 1], recv_sem=a_recv.at[q * (NY - 1) + e - 1],
            device_id=at_y(e), device_id_type=MESH,
        )

    def b_copy(q, e):
        return pltpu.make_async_remote_copy(
            src_ref=row_send.at[pl.ds(pl.multiple_of(q * SUB + lax.rem(z + e, NZ) * OWN, OWN), OWN)],
            dst_ref=row_recv.at[pl.ds(pl.multiple_of((q * (NZ - 1) + e - 1) * OWN, OWN), OWN)],
            send_sem=b_send.at[q * (NZ - 1) + e - 1], recv_sem=b_recv.at[q * (NZ - 1) + e - 1],
            device_id=at_z(e), device_id_type=MESH,
        )

    def d_copy(q, e, came=False):
        source = lax.rem(z + NZ - e, NZ) if came else z
        rows = pl.ds(pl.multiple_of(q * ROWS + OURS * SUB + source * OWN, OWN), OWN)
        return pltpu.make_async_remote_copy(
            src_ref=res_all.at[rows], dst_ref=res_all.at[rows],
            send_sem=d_send.at[q * (NZ - 1) + e - 1], recv_sem=d_recv.at[q * (NZ - 1) + e - 1],
            device_id=at_z(e), device_id_type=MESH,
        )

    def e_copy(q, e):
        return pltpu.make_async_remote_copy(
            src_ref=res_all.at[pl.ds(pl.multiple_of(q * ROWS + OURS * SUB, SUB), SUB)],
            dst_ref=res_all.at[pl.ds(pl.multiple_of(q * ROWS + SLOT_OF_SEND[e] * SUB, SUB), SUB)],
            send_sem=e_send.at[q * (NY - 1) + e - 1], recv_sem=e_recv.at[q * (NY - 1) + e - 1],
            device_id=at_y(e), device_id_type=MESH,
        )

    def step_0(q):
        part_send[a_rows(q, DELTAS[0]), :] = forward_step(q, 0, (q, 1, 2 * q)).astype(BF)

    def step_1(q):
        part_send[a_rows(q, DELTAS[1]), :] = forward_step(q, 1, (q, 2, 2 * q + 1)).astype(BF)

        @pl.when(q == 0)
        def _():
            pl.semaphore_wait(barrier, (NY - 1) + (NZ - 1) + len(group))

        a_copy(q, DELTAS[0]).start()
        a_copy(q, DELTAS[1]).start()

    def step_2(q):
        part_send[a_rows(q, DELTAS[2]), :] = forward_step(q, 2, (q, 3, 2 * q + 1)).astype(BF)
        a_copy(q, DELTAS[2]).start()

    def step_3(q):
        rows = pl.ds(pl.multiple_of(q * SUB, SUB), SUB)

        @pl.when(q < TILES - 1)
        def _():
            part_own[rows, :] = forward_step(q, 3, (q + 1, 0, 2 * q + 2))

        @pl.when(q == TILES - 1)
        def _():
            part_own[rows, :] = forward_step(q, 3)

    def sum_over_y(q):
        rows = pl.ds(pl.multiple_of(q * SUB, SUB), SUB)
        total = part_own[rows, :]
        for e in range(1, NY):
            a_copy(q, e).wait_recv()
        for e in range(1, NY):
            total = total + part_recv[a_rows(q, e), :].astype(F32)
        row_own[rows, :] = total
        row_send[rows, :] = total.astype(BF)
        for e in range(1, NZ):
            b_copy(q, e).start()

    def make_residual(q):
        total = row_own[pl.ds(pl.multiple_of(q * SUB + z * OWN, OWN), OWN), :]
        for e in range(1, NZ):
            b_copy(q, e).wait_recv()
        for e in range(1, NZ):
            at = pl.multiple_of((q * (NZ - 1) + e - 1) * OWN, OWN)
            total = total + row_recv[pl.ds(at, OWN), :].astype(F32)
        real, imag = -total[:, cases:], total[:, :cases]
        out_rows = pl.ds(pl.multiple_of(q * OWN, OWN), OWN)
        responses_ref[out_rows, :] = jnp.concatenate([real, imag], axis=1)
        magnitude = jnp.sqrt(real * real + imag * imag)
        weight = (magnitude - targets_ref[out_rows, :]) / jnp.maximum(magnitude, FLOOR)
        residual = jnp.concatenate([weight * real, weight * imag], axis=1).astype(BF)
        res_all[pl.ds(pl.multiple_of(q * ROWS + OURS * SUB + z * OWN, OWN), OWN), :] = residual
        for e in range(1, NZ):
            d_copy(q, e).start()

    def share_over_y(q):
        for e in range(1, NZ):
            d_copy(q, e, came=True).wait_recv()
        for e in range(1, NY):
            e_copy(q, e).start()

    def adjoint_sides(q, parity):
        pieces, t_pieces = [], []
        for j in (parity, parity + 2):
            at = pl.multiple_of(q * ROWS + j * SUB, SUB)
            pieces.append(res_all[pl.ds(at, SUB), :].astype(F32))
            t_pieces.append(t_rows[:, pl.ds(sub_row(q, j), SUB)])
        turned = jnp.concatenate(pieces, axis=0).T
        t_at = jnp.concatenate(t_pieces, axis=1)
        swapped = jnp.concatenate([turned[cases:], -turned[:cases]], axis=0)
        with_cos, with_sin = [swapped.astype(BF)], [turned.astype(BF)]
        for k in range(3):
            with_cos.append((swapped * t_at[k : k + 1, :]).astype(BF))
            with_sin.append((turned * t_at[k : k + 1, :]).astype(BF))
        return jnp.concatenate(with_cos, axis=0), jnp.concatenate(with_sin, axis=0)

    def adjoint_add(q, parity, sides, columns):
        cos_ref, sin_ref = ((cos_a, sin_a), (cos_b, sin_b))[parity]
        rows = pl.ds(pl.multiple_of(q * 2 * SUB, 2 * SUB), 2 * SUB)
        acc[:, columns] += jnp.dot(
            sides[0], cos_ref[rows, columns], preferred_element_type=F32
        ) + jnp.dot(sides[1], sin_ref[rows, columns], preferred_element_type=F32)

    first_sends = [e for e in SLOT_OF_SEND if SLOT_OF_SEND[e] % 2 == 1]
    other_sends = [e for e in SLOT_OF_SEND if SLOT_OF_SEND[e] % 2 == 0]

    def adjoint_tile(q):
        for parity, sends in ((1, first_sends), (0, other_sends)):
            for e in sends:
                e_copy(q, e).wait_recv()
            adjoint_add(q, parity, adjoint_sides(q, parity), slice(0, patches))

    for begin in range(0, SUB, quarter):
        trig_piece(0, 0, cos_a, sin_a, 0, begin, quarter)
    fetch.wait()
    targets_ref[...] = targets_t[...].T

    def step(it, carry):
        def when(work, lag):
            inside = jnp.logical_and(it >= lag, it < TILES + lag)
            pl.when(inside)(lambda: work(it - lag))

        when(step_0, 0)
        when(step_1, 0)
        when(make_residual, 3)
        when(step_2, 0)
        when(step_3, 0)
        when(share_over_y, 4)
        when(sum_over_y, 1)
        pl.when(it >= 6)(lambda: adjoint_tile(it - 6))
        return carry

    lax.fori_loop(0, TILES + 5, step, 0)

    half = 2 * cases
    share = half // NX
    cuts = (slice(0, 512), slice(512, patches))
    last = TILES - 1

    def gradient(which, columns):
        if which == 0:
            return acc[0:half, columns] * scale_row[:, columns]
        total = acc[half : 2 * half, columns] * face_rows[0:1, columns]
        for k in range(1, 3):
            begin = (k + 1) * half
            total = total + acc[begin : begin + half, columns] * face_rows[k : k + 1, columns]
        return total * scale_row[:, columns]

    def g_copy(n):
        return pltpu.make_async_remote_copy(
            src_ref=half_send.at[:, cuts[n]], dst_ref=half_recv.at[:, cuts[n]],
            send_sem=g_send.at[n], recv_sem=g_recv.at[n],
            device_id=at_dir(0, 1), device_id_type=MESH,
        )

    def h_copy(n, e):
        source = pl.ds(pl.multiple_of(lax.rem(x + e, NX) * share, share), share)
        return pltpu.make_async_remote_copy(
            src_ref=quarter_send.at[source, cuts[n]],
            dst_ref=quarter_recv.at[pl.ds((e - 1) * share, share), cuts[n]],
            send_sem=h_send.at[3 * n + e - 1], recv_sem=h_recv.at[3 * n + e - 1],
            device_id=at_dir(e, 0), device_id_type=MESH,
        )

    def place(ex, ec):
        at = lax.rem(core + ec, 2) * half + lax.rem(x + NX - ex, NX) * share
        return pl.ds(pl.multiple_of(at, share), share)

    def k_copy(n, e, came=False):
        rows = place(e, 0) if came else place(0, 0)
        return pltpu.make_async_remote_copy(
            src_ref=grad_all.at[rows, cuts[n]], dst_ref=grad_all.at[rows, cuts[n]],
            send_sem=k_send.at[3 * n + e - 1], recv_sem=k_recv.at[3 * n + e - 1],
            device_id=at_dir(e, 0), device_id_type=MESH,
        )

    def m_copy(n, e, came=False):
        rows = place(e, 1) if came else place(e, 0)
        return pltpu.make_async_remote_copy(
            src_ref=grad_all.at[rows, cuts[n]], dst_ref=grad_all.at[rows, cuts[n]],
            send_sem=m_send.at[NX * n + e], recv_sem=m_recv.at[NX * n + e],
            device_id=at_dir(0, 1), device_id_type=MESH,
        )

    for e in first_sends:
        e_copy(last, e).wait_recv()
    adjoint_add(last, 1, adjoint_sides(last, 1), slice(0, patches))
    for e in other_sends:
        e_copy(last, e).wait_recv()
    sides = adjoint_sides(last, 0)
    for n, columns in enumerate(cuts):
        adjoint_add(last, 0, sides, columns)
        for which in range(2):
            grad = gradient(which, columns)

            @pl.when(core == which)
            def _():
                quarter_own[:, columns] = grad

            @pl.when(core != which)
            def _():
                half_send[:, columns] = grad.astype(BF)

        g_copy(n).start()
    for n, columns in enumerate(cuts):
        g_copy(n).wait_recv()
        chip = quarter_own[:, columns] + half_recv[:, columns].astype(F32)
        quarter_own[:, columns] = chip
        quarter_send[:, columns] = chip.astype(BF)
        for e in (2, 1, 3):
            h_copy(n, e).start()
    for n, columns in enumerate(cuts):
        total = quarter_own[pl.ds(pl.multiple_of(x * share, share), share), columns]
        for e in range(1, NX):
            h_copy(n, e).wait_recv()
        for e in range(1, NX):
            total = total + quarter_recv[(e - 1) * share : e * share, columns].astype(F32)
        grad_all[place(0, 0), columns] = total.astype(BF)
        for e in (2, 1, 3):
            k_copy(n, e).start()
        m_copy(n, 0).start()
    for n in range(2):
        for e in (1, 3, 2):
            k_copy(n, e, came=True).wait_recv()
            m_copy(n, e).start()
    for n in range(2):
        for e in range(NX):
            m_copy(n, e, came=True).wait_recv()
    grads_ref[...] = grad_all[...]

    for n in range(2):
        g_copy(n).wait_send()
        for e in range(1, NX):
            h_copy(n, e).wait_send()
            k_copy(n, e).wait_send()
        for e in range(NX):
            m_copy(n, e).wait_send()

    def drain(q, carry):
        for e in range(1, NY):
            a_copy(q, e).wait_send()
            e_copy(q, e).wait_send()
        for e in range(1, NZ):
            b_copy(q, e).wait_send()
            d_copy(q, e).wait_send()
        return carry

    lax.fori_loop(0, TILES, drain, 0)


def finish(responses_ref, grads_ref, out_ref, grad_p_ref, grad_v_ref):
    half = grads_ref.shape[0] // 2
    out_ref[...] = responses_ref[...]
    grad_v_ref[...] = grads_ref[0:half, :].astype(F32).T
    grad_p_ref[...] = grads_ref[half : 2 * half, :].astype(F32).T


def shards(direction_angles, positions, normal_angles, areas, pressure, velocity, targets):
    cases = targets.shape[1]
    patches = positions.shape[1]
    dirs = direction_angles.shape[1]
    total_patches = patches * lax.axis_size("surf")
    owners = NY * NZ
    vmem = pl.BlockSpec(memory_space=pltpu.VMEM)
    half = 2 * cases
    dma = pltpu.SemaphoreType.DMA
    slots = 2 * TILES
    responses, grads = pl.pallas_call(
        functools.partial(body, total_patches),
        out_shape=(
            jax.ShapeDtypeStruct((dirs // owners, half), F32),
            jax.ShapeDtypeStruct((2 * half, patches), BF),
        ),
        in_specs=[vmem] * 6 + [pl.BlockSpec(memory_space=pl.ANY)],
        out_specs=(vmem, vmem),
        scratch_shapes=[
            pltpu.VMEM((cases, TILES * OWN), F32),
            pltpu.VMEM((TILES * OWN, cases), F32),
            pltpu.VMEM((8, dirs), F32),
            pltpu.VMEM((dirs, 8), F32),
            pltpu.VMEM((dirs, 8), F32),
            pltpu.VMEM((32, dirs), F32),
            pltpu.VMEM((32, patches), F32),
            pltpu.VMEM((8, dirs), F32),
            pltpu.VMEM((dirs, 8), F32),
            pltpu.VMEM((dirs, 32), BF),
            pltpu.VMEM((32, patches), BF),
            pltpu.VMEM((8, patches), F32),
            pltpu.VMEM((2 * patches, 4 * half), BF),
            pltpu.VMEM((slots * SUB, patches), BF),
            pltpu.VMEM((slots * SUB, patches), BF),
            pltpu.VMEM((slots * SUB, patches), BF),
            pltpu.VMEM((slots * SUB, patches), BF),
            pltpu.VMEM((TILES * (NY - 1) * SUB, half), BF),
            pltpu.VMEM((TILES * (NY - 1) * SUB, half), BF),
            pltpu.VMEM((TILES * SUB, half), F32),
            pltpu.VMEM((TILES * SUB, half), F32),
            pltpu.VMEM((TILES * SUB, half), BF),
            pltpu.VMEM((TILES * (NZ - 1) * OWN, half), BF),
            pltpu.VMEM((TILES * ROWS, half), BF),
            pltpu.VMEM((4 * half, patches), F32),
            pltpu.VMEM((half, patches), BF),
            pltpu.VMEM((half, patches), BF),
            pltpu.VMEM((half, patches), F32),
            pltpu.VMEM((half, patches), BF),
            pltpu.VMEM((half // NX * (NX - 1), patches), BF),
            pltpu.VMEM((2 * half, patches), BF),
            dma,
            dma((TILES * (NY - 1),)), dma((TILES * (NY - 1),)),
            dma((TILES * (NZ - 1),)), dma((TILES * (NZ - 1),)),
            dma((TILES * (NZ - 1),)), dma((TILES * (NZ - 1),)),
            dma((TILES * (NY - 1),)), dma((TILES * (NY - 1),)),
            dma((2,)), dma((2,)),
            dma((2 * (NX - 1),)), dma((2 * (NX - 1),)),
            dma((2 * (NX - 1),)), dma((2 * (NX - 1),)),
            dma((2 * NX,)), dma((2 * NX,)),
        ],
        compiler_params=pltpu.CompilerParams(
            collective_id=0, has_side_effects=True, vmem_limit_bytes=56 * 2**20
        ),
    )(
        direction_angles, positions, normal_angles, areas.reshape(patches // 128, 128),
        pressure, velocity, targets.T,
    )
    return pl.pallas_call(
        finish,
        out_shape=(
            jax.ShapeDtypeStruct((dirs // owners, half), F32),
            jax.ShapeDtypeStruct((patches, half), F32),
            jax.ShapeDtypeStruct((patches, half), F32),
        ),
        in_specs=[vmem] * 2,
        out_specs=(vmem, vmem, vmem),
    )(responses, grads)


def solution(mesh):
    in_specs = (
        P(None, "dir"),
        P(None, "surf"),
        P(None, "surf"),
        P("surf"),
        P("surf", None),
        P("surf", None),
        P("dir", None),
    )
    out_specs = (P(("dir", "surf"), None), P("surf", None), P("surf", None))
    return jax.shard_map(shards, mesh=mesh, in_specs=in_specs, out_specs=out_specs, check_vma=False)
```

```python
import functools
import math

import jax
import jax.numpy as jnp
from jax import lax
from jax.experimental import pallas as pl
from jax.experimental.pallas import tpu as pltpu
from jax.sharding import PartitionSpec as P

MESH = pl.DeviceIdType.MESH
BF = jnp.bfloat16
F32 = jnp.float32
FLOOR = 0.5

TILES = 4
NY, NZ, NX = 4, 8, 4
OWN = 32
SUB = NZ * OWN
ROWS = NY * SUB
DELTAS = (2, 1, 3, 0)
FAR_FIRST = (4, 3, 5, 2, 6, 1, 7)
OURS = 3
SLOT_OF_SEND = {1: 2, 2: 0, 3: 1}

ROOT2 = math.sqrt(2.0)
SIN_HALF = [c * ROOT2 for c in (3.14158198, -5.1671413, 2.54188707, -0.55460885)]
SIN_FINE = [c * ROOT2 for c in (3.14159258, -5.16770687, 2.55003119, -0.59804419, 0.07721839)]
COS_FINE = [c * ROOT2 for c in (0.99999995, -4.93479283, 4.05841135, -1.33187657, 0.21968961)]


def horner(coefficients, square):
    value = coefficients[-1]
    for coefficient in coefficients[-2::-1]:
        value = value * square + coefficient
    return value


def cos_sin(cycles):
    rest = cycles - jnp.round(cycles)
    half_sine = horner(SIN_HALF, rest * rest) * rest
    double = half_sine * half_sine
    left = jnp.maximum(2.0 - double, 1e-20)
    return 1.0 - double, half_sine * (left * lax.rsqrt(left))


def fine_cos_sin(angle):
    cycles = angle * F32(1.0 / (2.0 * math.pi))
    rest = cycles - jnp.round(cycles)
    square = rest * rest
    half_sine = horner(SIN_FINE, square) * rest
    return 1.0 - half_sine * half_sine, half_sine * horner(COS_FINE, square)


def unit_rows(angles):
    cos_all, sin_all = fine_cos_sin(angles)
    cos_polar, sin_polar = cos_all[0:1], sin_all[0:1]
    cos_azimuth, sin_azimuth = cos_all[1:2], sin_all[1:2]
    return sin_polar * cos_azimuth, sin_polar * sin_azimuth, cos_polar


def three_parts(value):
    first = value.astype(BF).astype(F32)
    second = (value - first).astype(BF).astype(F32)
    return first, second, value - first - second


def body(
    total_patches,
    angles_ref, positions_ref, normals_ref, areas_ref, pressure_hbm, velocity_hbm, targets_hbm,
    responses_ref, grads_ref,
    pressure_ref, velocity_ref, targets_t, targets_ref, angle_rows, angle_cols, angle_perm, split_t, split_x, t_rows, t_cols, t_lhs, x_rhs, face_rows, weights,
    cos_a, sin_a, cos_b, sin_b,
    part_send, part_recv, part_own, row_own, row_send, row_recv, res_all, acc,
    half_send, half_recv, quarter_own, quarter_send, quarter_recv, grad_all,
    local_sem, a_send, a_recv, b_send, b_recv, d_send, d_recv,
    e_send, e_recv,
    g_send, g_recv, h_send, h_recv, k_send, k_recv, m_send, m_recv,
):
    dir_index = lax.axis_index("dir")
    surf_index = lax.axis_index("surf")
    x, core = dir_index // 2, lax.rem(dir_index, 2)
    y, z = surf_index // NZ, lax.rem(surf_index, NZ)
    patches = positions_ref.shape[1]

    def at_y(e):
        return (dir_index, lax.rem(y + e, NY) * NZ + z)

    def at_z(e):
        return (dir_index, y * NZ + lax.rem(z + e, NZ))

    def at_dir(ex, ec):
        return (lax.rem(x + ex, NX) * 2 + lax.rem(core + ec, 2), surf_index)

    group = [(ex, 0) for ex in range(1, NX)] + [(0, 1)]
    barrier = pltpu.get_barrier_semaphore()
    for e in range(1, NY):
        pl.semaphore_signal(barrier, inc=1, device_id=at_y(e), device_id_type=MESH)
    for e in range(1, NZ):
        pl.semaphore_signal(barrier, inc=1, device_id=at_z(e), device_id_type=MESH)
    for ex, ec in group:
        pl.semaphore_signal(barrier, inc=1, device_id=at_dir(ex, ec), device_id_type=MESH)

    own_rows = TILES * OWN
    fetch = pltpu.make_async_copy(
        targets_hbm.at[:, pl.ds(pl.multiple_of(surf_index * own_rows, own_rows), own_rows)],
        targets_t, local_sem.at[0],
    )
    fetch_p = pltpu.make_async_copy(pressure_hbm, pressure_ref, local_sem.at[1])
    fetch_v = pltpu.make_async_copy(velocity_hbm, velocity_ref, local_sem.at[2])
    fetch_p.start()
    fetch_v.start()
    fetch.start()

    angle_rows[...] = jnp.zeros_like(angle_rows)
    angle_rows[0:2, :] = angles_ref[...]
    angle_cols[...] = angle_rows[...].T
    for q in range(TILES):
        for owner in range(NY * NZ):
            begin, source = q * ROWS + owner * OWN, owner * own_rows + q * OWN
            angle_perm[begin : begin + OWN, :] = angle_cols[source : source + OWN, :]
    tx, ty, tz = unit_rows(angle_perm[...].T)
    split_t[...] = jnp.zeros_like(split_t)
    split_x[...] = jnp.zeros_like(split_x)
    t_rows[...] = jnp.zeros_like(t_rows)
    for k, row in enumerate((tx, ty, tz)):
        t_rows[k : k + 1, :] = row
        first, second, third = three_parts(row)
        for at, part in enumerate((first, first, second, second, first, third)):
            split_t[3 * at + k : 3 * at + k + 1, :] = part
        first, second, third = three_parts(positions_ref[k : k + 1, :] * F32(0.5 / math.pi))
        for at, part in enumerate((first, second, first, second, third, first)):
            split_x[3 * at + k : 3 * at + k + 1, :] = part
    x_rhs[...] = split_x[...].astype(BF)
    t_lhs[...] = split_t[...].T.astype(BF)
    t_cols[...] = t_rows[...].T

    face_rows[...] = jnp.zeros_like(face_rows)
    for at in range(areas_ref.shape[0]):
        face_rows[3:4, 128 * at : 128 * (at + 1)] = areas_ref[at : at + 1, :]
    scale_row = face_rows[3:4, :] * F32(1.0 / math.sqrt(total_patches))
    for k, row in enumerate(unit_rows(normals_ref[...])):
        face_rows[k : k + 1, :] = row
    face_rows[3:4, :] = scale_row
    face_cols = face_rows[...].T
    scale_col = face_cols[:, 3:4]
    fetch_p.wait()
    fetch_v.wait()
    weighted_p = (pressure_ref[...].astype(F32) * scale_col).astype(BF).astype(F32)
    weighted_v = (velocity_ref[...].astype(F32) * scale_col).astype(BF).astype(F32)
    cases = weighted_p.shape[1] // 2
    for k in range(4):
        source = weighted_v if k == 0 else weighted_p * face_cols[:, k - 1 : k]
        turned = jnp.concatenate([source[:, cases:], -source[:, :cases]], axis=1)
        columns = slice(k * 2 * cases, (k + 1) * 2 * cases)
        weights[0:patches, columns] = source.astype(BF)
        weights[patches : 2 * patches, columns] = turned.astype(BF)
    acc[...] = jnp.zeros_like(acc)

    def sub_row(q, j):
        return pl.multiple_of(q * ROWS + lax.rem(y + DELTAS[j], NY) * SUB, SUB)

    def trig_piece(q, j, cos_ref, sin_ref, slot, begin, count):
        angle = jnp.dot(
            t_lhs[pl.ds(sub_row(q, j) + begin, count), :], x_rhs[...], preferred_element_type=F32
        )
        cosine, sine = cos_sin(angle)
        at = pl.multiple_of(slot * SUB + begin, count)
        cos_ref[pl.ds(at, count), :] = cosine.astype(BF)
        sin_ref[pl.ds(at, count), :] = sine.astype(BF)

    quarter = SUB // 4

    def forward_step(q, j, after=None):
        def make(piece):
            if after is not None:
                tq, tj, slot = after
                tc, ts = (cos_a, sin_a) if tj % 2 == 0 else (cos_b, sin_b)
                trig_piece(tq, tj, tc, ts, slot, piece * quarter, quarter)

        mc, ms = (cos_a, sin_a) if j % 2 == 0 else (cos_b, sin_b)
        rows = pl.ds(pl.multiple_of((2 * q + j // 2) * SUB, SUB), SUB)
        halves = []
        for h in range(2):
            columns = slice(4 * cases * h, 4 * cases * (h + 1))
            g = jnp.dot(mc[rows, :], weights[0:patches, columns], preferred_element_type=F32)
            make(2 * h)
            g = g + jnp.dot(
                ms[rows, :], weights[patches : 2 * patches, columns], preferred_element_type=F32
            )
            make(2 * h + 1)
            halves.append(g)
        t_at = t_cols[pl.ds(sub_row(q, j), SUB), :]
        lo, hi = halves
        return (
            lo[:, : 2 * cases]
            + t_at[:, 0:1] * lo[:, 2 * cases :]
            + t_at[:, 1:2] * hi[:, : 2 * cases]
            + t_at[:, 2:3] * hi[:, 2 * cases :]
        )

    def a_rows(q, e):
        return pl.ds(pl.multiple_of((q * (NY - 1) + e - 1) * SUB, SUB), SUB)

    def a_copy(q, e):
        return pltpu.make_async_remote_copy(
            src_ref=part_send.at[a_rows(q, e)], dst_ref=part_recv.at[a_rows(q, e)],
            send_sem=a_send.at[q * (NY - 1) + e - 1], recv_sem=a_recv.at[q * (NY - 1) + e - 1],
            device_id=at_y(e), device_id_type=MESH,
        )

    def b_copy(q, e):
        return pltpu.make_async_remote_copy(
            src_ref=row_send.at[pl.ds(pl.multiple_of(q * SUB + lax.rem(z + e, NZ) * OWN, OWN), OWN)],
            dst_ref=row_recv.at[pl.ds(pl.multiple_of((q * (NZ - 1) + e - 1) * OWN, OWN), OWN)],
            send_sem=b_send.at[q * (NZ - 1) + e - 1], recv_sem=b_recv.at[q * (NZ - 1) + e - 1],
            device_id=at_z(e), device_id_type=MESH,
        )

    def d_copy(q, e, came=False):
        source = lax.rem(z + NZ - e, NZ) if came else z
        rows = pl.ds(pl.multiple_of(q * ROWS + OURS * SUB + source * OWN, OWN), OWN)
        return pltpu.make_async_remote_copy(
            src_ref=res_all.at[rows], dst_ref=res_all.at[rows],
            send_sem=d_send.at[q * (NZ - 1) + e - 1], recv_sem=d_recv.at[q * (NZ - 1) + e - 1],
            device_id=at_z(e), device_id_type=MESH,
        )

    def e_copy(q, e):
        return pltpu.make_async_remote_copy(
            src_ref=res_all.at[pl.ds(pl.multiple_of(q * ROWS + OURS * SUB, SUB), SUB)],
            dst_ref=res_all.at[pl.ds(pl.multiple_of(q * ROWS + SLOT_OF_SEND[e] * SUB, SUB), SUB)],
            send_sem=e_send.at[q * (NY - 1) + e - 1], recv_sem=e_recv.at[q * (NY - 1) + e - 1],
            device_id=at_y(e), device_id_type=MESH,
        )

    def step_0(q):
        part_send[a_rows(q, DELTAS[0]), :] = forward_step(q, 0, (q, 1, 2 * q)).astype(BF)

    def step_1(q):
        part_send[a_rows(q, DELTAS[1]), :] = forward_step(q, 1, (q, 2, 2 * q + 1)).astype(BF)

        @pl.when(q == 0)
        def _():
            pl.semaphore_wait(barrier, (NY - 1) + (NZ - 1) + len(group))

        a_copy(q, DELTAS[0]).start()
        a_copy(q, DELTAS[1]).start()

    def step_2(q):
        part_send[a_rows(q, DELTAS[2]), :] = forward_step(q, 2, (q, 3, 2 * q + 1)).astype(BF)
        a_copy(q, DELTAS[2]).start()

    def step_3(q):
        rows = pl.ds(pl.multiple_of(q * SUB, SUB), SUB)

        @pl.when(q < TILES - 1)
        def _():
            part_own[rows, :] = forward_step(q, 3, (q + 1, 0, 2 * q + 2))

        @pl.when(q == TILES - 1)
        def _():
            part_own[rows, :] = forward_step(q, 3)

    def sum_over_y(q):
        rows = pl.ds(pl.multiple_of(q * SUB, SUB), SUB)
        total = part_own[rows, :]
        for e in range(1, NY):
            a_copy(q, e).wait_recv()
        for e in range(1, NY):
            total = total + part_recv[a_rows(q, e), :].astype(F32)
        row_own[rows, :] = total
        row_send[rows, :] = total.astype(BF)
        for e in FAR_FIRST:
            b_copy(q, e).start()

    def make_residual(q):
        total = row_own[pl.ds(pl.multiple_of(q * SUB + z * OWN, OWN), OWN), :]
        for e in range(1, NZ):
            b_copy(q, e).wait_recv()
        for e in range(1, NZ):
            at = pl.multiple_of((q * (NZ - 1) + e - 1) * OWN, OWN)
            total = total + row_recv[pl.ds(at, OWN), :].astype(F32)
        real, imag = -total[:, cases:], total[:, :cases]
        out_rows = pl.ds(pl.multiple_of(q * OWN, OWN), OWN)
        responses_ref[out_rows, :] = jnp.concatenate([real, imag], axis=1)
        magnitude = jnp.sqrt(real * real + imag * imag)
        weight = (magnitude - targets_ref[out_rows, :]) / jnp.maximum(magnitude, FLOOR)
        residual = jnp.concatenate([weight * real, weight * imag], axis=1).astype(BF)
        res_all[pl.ds(pl.multiple_of(q * ROWS + OURS * SUB + z * OWN, OWN), OWN), :] = residual
        for e in FAR_FIRST:
            d_copy(q, e).start()

    def share_over_y(q):
        for e in range(1, NZ):
            d_copy(q, e, came=True).wait_recv()
        for e in (2, 1, 3):
            e_copy(q, e).start()

    def adjoint_sides(q, parity):
        pieces, t_pieces = [], []
        for j in (parity, parity + 2):
            at = pl.multiple_of(q * ROWS + j * SUB, SUB)
            pieces.append(res_all[pl.ds(at, SUB), :].astype(F32))
            t_pieces.append(t_rows[:, pl.ds(sub_row(q, j), SUB)])
        turned = jnp.concatenate(pieces, axis=0).T
        t_at = jnp.concatenate(t_pieces, axis=1)
        swapped = jnp.concatenate([turned[cases:], -turned[:cases]], axis=0)
        with_cos, with_sin = [swapped.astype(BF)], [turned.astype(BF)]
        for k in range(3):
            with_cos.append((swapped * t_at[k : k + 1, :]).astype(BF))
            with_sin.append((turned * t_at[k : k + 1, :]).astype(BF))
        return jnp.concatenate(with_cos, axis=0), jnp.concatenate(with_sin, axis=0)

    def adjoint_add(q, parity, sides, columns):
        cos_ref, sin_ref = ((cos_a, sin_a), (cos_b, sin_b))[parity]
        rows = pl.ds(pl.multiple_of(q * 2 * SUB, 2 * SUB), 2 * SUB)
        acc[:, columns] += jnp.dot(
            sides[0], cos_ref[rows, columns], preferred_element_type=F32
        ) + jnp.dot(sides[1], sin_ref[rows, columns], preferred_element_type=F32)

    first_sends = [e for e in SLOT_OF_SEND if SLOT_OF_SEND[e] % 2 == 1]
    other_sends = [e for e in SLOT_OF_SEND if SLOT_OF_SEND[e] % 2 == 0]

    def adjoint_tile(q):
        for parity, sends in ((1, first_sends), (0, other_sends)):
            for e in sends:
                e_copy(q, e).wait_recv()
            adjoint_add(q, parity, adjoint_sides(q, parity), slice(0, patches))

    for begin in range(0, SUB, quarter):
        trig_piece(0, 0, cos_a, sin_a, 0, begin, quarter)
    fetch.wait()
    targets_ref[...] = targets_t[...].T

    def step(it, carry):
        def when(work, lag):
            inside = jnp.logical_and(it >= lag, it < TILES + lag)
            pl.when(inside)(lambda: work(it - lag))

        when(step_0, 0)
        when(step_1, 0)
        when(make_residual, 3)
        when(step_2, 0)
        when(step_3, 0)
        when(sum_over_y, 1)
        pl.when(it >= 6)(lambda: adjoint_tile(it - 6))
        when(share_over_y, 4)
        return carry

    lax.fori_loop(0, TILES + 5, step, 0)

    half = 2 * cases
    share = half // NX
    cuts = (slice(0, 512), slice(512, patches))
    last = TILES - 1

    def gradient(which, columns):
        if which == 0:
            return acc[0:half, columns] * scale_row[:, columns]
        total = acc[half : 2 * half, columns] * face_rows[0:1, columns]
        for k in range(1, 3):
            begin = (k + 1) * half
            total = total + acc[begin : begin + half, columns] * face_rows[k : k + 1, columns]
        return total * scale_row[:, columns]

    def g_copy(n):
        return pltpu.make_async_remote_copy(
            src_ref=half_send.at[:, cuts[n]], dst_ref=half_recv.at[:, cuts[n]],
            send_sem=g_send.at[n], recv_sem=g_recv.at[n],
            device_id=at_dir(0, 1), device_id_type=MESH,
        )

    def h_copy(n, e):
        source = pl.ds(pl.multiple_of(lax.rem(x + e, NX) * share, share), share)
        return pltpu.make_async_remote_copy(
            src_ref=quarter_send.at[source, cuts[n]],
            dst_ref=quarter_recv.at[pl.ds((e - 1) * share, share), cuts[n]],
            send_sem=h_send.at[3 * n + e - 1], recv_sem=h_recv.at[3 * n + e - 1],
            device_id=at_dir(e, 0), device_id_type=MESH,
        )

    def place(ex, ec):
        at = lax.rem(core + ec, 2) * half + lax.rem(x + NX - ex, NX) * share
        return pl.ds(pl.multiple_of(at, share), share)

    def k_copy(n, e, came=False):
        rows = place(e, 0) if came else place(0, 0)
        return pltpu.make_async_remote_copy(
            src_ref=grad_all.at[rows, cuts[n]], dst_ref=grad_all.at[rows, cuts[n]],
            send_sem=k_send.at[3 * n + e - 1], recv_sem=k_recv.at[3 * n + e - 1],
            device_id=at_dir(e, 0), device_id_type=MESH,
        )

    def m_copy(n, e, came=False):
        rows = place(e, 1) if came else place(e, 0)
        return pltpu.make_async_remote_copy(
            src_ref=grad_all.at[rows, cuts[n]], dst_ref=grad_all.at[rows, cuts[n]],
            send_sem=m_send.at[NX * n + e], recv_sem=m_recv.at[NX * n + e],
            device_id=at_dir(0, 1), device_id_type=MESH,
        )

    for e in first_sends:
        e_copy(last, e).wait_recv()
    adjoint_add(last, 1, adjoint_sides(last, 1), slice(0, patches))
    for e in other_sends:
        e_copy(last, e).wait_recv()
    sides = adjoint_sides(last, 0)
    for n, columns in enumerate(cuts):
        adjoint_add(last, 0, sides, columns)
        for which in range(2):
            grad = gradient(which, columns)

            @pl.when(core == which)
            def _():
                quarter_own[:, columns] = grad

            @pl.when(core != which)
            def _():
                half_send[:, columns] = grad.astype(BF)

        g_copy(n).start()
    def drain(q, carry):
        for e in range(1, NY):
            a_copy(q, e).wait_send()
            e_copy(q, e).wait_send()
        for e in range(1, NZ):
            b_copy(q, e).wait_send()
            d_copy(q, e).wait_send()
        return carry

    for n, columns in enumerate(cuts):
        g_copy(n).wait_recv()
        chip = quarter_own[:, columns] + half_recv[:, columns].astype(F32)
        quarter_own[:, columns] = chip
        quarter_send[:, columns] = chip.astype(BF)
        for e in (2, 1, 3):
            h_copy(n, e).start()
    lax.fori_loop(0, TILES, drain, 0)
    for n, columns in enumerate(cuts):
        total = quarter_own[pl.ds(pl.multiple_of(x * share, share), share), columns]
        for e in range(1, NX):
            h_copy(n, e).wait_recv()
        for e in range(1, NX):
            total = total + quarter_recv[(e - 1) * share : e * share, columns].astype(F32)
        grad_all[place(0, 0), columns] = total.astype(BF)
        for e in (2, 1, 3):
            k_copy(n, e).start()
        m_copy(n, 0).start()
    for n in range(2):
        g_copy(n).wait_send()
        for e in range(1, NX):
            h_copy(n, e).wait_send()
    for n in range(2):
        for e in (1, 3, 2):
            k_copy(n, e, came=True).wait_recv()
            m_copy(n, e).start()
    for n in range(2):
        for e in range(1, NX):
            k_copy(n, e).wait_send()
        for e in range(NX):
            m_copy(n, e, came=True).wait_recv()
    grads_ref[...] = grad_all[...]
    for n in range(2):
        for e in range(NX):
            m_copy(n, e).wait_send()


def finish(responses_ref, grads_ref, out_ref, grad_p_ref, grad_v_ref):
    half = grads_ref.shape[0] // 2
    out_ref[...] = responses_ref[...]
    grad_v_ref[...] = grads_ref[0:half, :].astype(F32).T
    grad_p_ref[...] = grads_ref[half : 2 * half, :].astype(F32).T


def shards(direction_angles, positions, normal_angles, areas, pressure, velocity, targets):
    cases = targets.shape[1]
    patches = positions.shape[1]
    dirs = direction_angles.shape[1]
    total_patches = patches * lax.axis_size("surf")
    owners = NY * NZ
    vmem = pl.BlockSpec(memory_space=pltpu.VMEM)
    half = 2 * cases
    dma = pltpu.SemaphoreType.DMA
    slots = 2 * TILES
    responses, grads = pl.pallas_call(
        functools.partial(body, total_patches),
        out_shape=(
            jax.ShapeDtypeStruct((dirs // owners, half), F32),
            jax.ShapeDtypeStruct((2 * half, patches), BF),
        ),
        in_specs=[vmem] * 4 + [pl.BlockSpec(memory_space=pl.ANY)] * 3,
        out_specs=(vmem, vmem),
        scratch_shapes=[
            pltpu.VMEM((patches, half), BF),
            pltpu.VMEM((patches, half), BF),
            pltpu.VMEM((cases, TILES * OWN), F32),
            pltpu.VMEM((TILES * OWN, cases), F32),
            pltpu.VMEM((8, dirs), F32),
            pltpu.VMEM((dirs, 8), F32),
            pltpu.VMEM((dirs, 8), F32),
            pltpu.VMEM((32, dirs), F32),
            pltpu.VMEM((32, patches), F32),
            pltpu.VMEM((8, dirs), F32),
            pltpu.VMEM((dirs, 8), F32),
            pltpu.VMEM((dirs, 32), BF),
            pltpu.VMEM((32, patches), BF),
            pltpu.VMEM((8, patches), F32),
            pltpu.VMEM((2 * patches, 4 * half), BF),
            pltpu.VMEM((slots * SUB, patches), BF),
            pltpu.VMEM((slots * SUB, patches), BF),
            pltpu.VMEM((slots * SUB, patches), BF),
            pltpu.VMEM((slots * SUB, patches), BF),
            pltpu.VMEM((TILES * (NY - 1) * SUB, half), BF),
            pltpu.VMEM((TILES * (NY - 1) * SUB, half), BF),
            pltpu.VMEM((TILES * SUB, half), F32),
            pltpu.VMEM((TILES * SUB, half), F32),
            pltpu.VMEM((TILES * SUB, half), BF),
            pltpu.VMEM((TILES * (NZ - 1) * OWN, half), BF),
            pltpu.VMEM((TILES * ROWS, half), BF),
            pltpu.VMEM((4 * half, patches), F32),
            pltpu.VMEM((half, patches), BF),
            pltpu.VMEM((half, patches), BF),
            pltpu.VMEM((half, patches), F32),
            pltpu.VMEM((half, patches), BF),
            pltpu.VMEM((half // NX * (NX - 1), patches), BF),
            pltpu.VMEM((2 * half, patches), BF),
            dma((3,)),
            dma((TILES * (NY - 1),)), dma((TILES * (NY - 1),)),
            dma((TILES * (NZ - 1),)), dma((TILES * (NZ - 1),)),
            dma((TILES * (NZ - 1),)), dma((TILES * (NZ - 1),)),
            dma((TILES * (NY - 1),)), dma((TILES * (NY - 1),)),
            dma((2,)), dma((2,)),
            dma((2 * (NX - 1),)), dma((2 * (NX - 1),)),
            dma((2 * (NX - 1),)), dma((2 * (NX - 1),)),
            dma((2 * NX,)), dma((2 * NX,)),
        ],
        compiler_params=pltpu.CompilerParams(
            collective_id=0, has_side_effects=True, vmem_limit_bytes=56 * 2**20
        ),
    )(
        direction_angles, positions, normal_angles, areas.reshape(patches // 128, 128),
        pressure, velocity, targets.T,
    )
    return pl.pallas_call(
        finish,
        out_shape=(
            jax.ShapeDtypeStruct((dirs // owners, half), F32),
            jax.ShapeDtypeStruct((patches, half), F32),
            jax.ShapeDtypeStruct((patches, half), F32),
        ),
        in_specs=[vmem] * 2,
        out_specs=(vmem, vmem, vmem),
    )(responses, grads)


def solution(mesh):
    in_specs = (
        P(None, "dir"),
        P(None, "surf"),
        P(None, "surf"),
        P("surf"),
        P("surf", None),
        P("surf", None),
        P("dir", None),
    )
    out_specs = (P(("dir", "surf"), None), P("surf", None), P("surf", None))
    return jax.shard_map(shards, mesh=mesh, in_specs=in_specs, out_specs=out_specs, check_vma=False)
```

```python
import functools
import math

import jax
import jax.numpy as jnp
from jax import lax
from jax.experimental import pallas as pl
from jax.experimental.pallas import tpu as pltpu
from jax.sharding import PartitionSpec as P

MESH = pl.DeviceIdType.MESH
BF = jnp.bfloat16
F32 = jnp.float32
FLOOR = 0.5

TILES = 4
NY, NZ, NX = 4, 8, 4
OWN = 32
SUB = NZ * OWN
ROWS = NY * SUB
DELTAS = (2, 1, 3, 0)
FAR_FIRST = (4, 3, 5, 2, 6, 1, 7)
OURS = 3
SLOT_OF_SEND = {1: 2, 2: 0, 3: 1}

ROOT2 = math.sqrt(2.0)
SIN_HALF = [c * ROOT2 for c in (3.14158198, -5.1671413, 2.54188707, -0.55460885)]
SIN_FINE = [c * ROOT2 for c in (3.14159258, -5.16770687, 2.55003119, -0.59804419, 0.07721839)]
COS_FINE = [c * ROOT2 for c in (0.99999995, -4.93479283, 4.05841135, -1.33187657, 0.21968961)]


def horner(coefficients, square):
    value = coefficients[-1]
    for coefficient in coefficients[-2::-1]:
        value = value * square + coefficient
    return value


def cos_sin(cycles):
    rest = cycles - jnp.round(cycles)
    half_sine = horner(SIN_HALF, rest * rest) * rest
    double = half_sine * half_sine
    left = jnp.maximum(2.0 - double, 1e-20)
    return 1.0 - double, half_sine * (left * lax.rsqrt(left))


def fine_cos_sin(angle):
    cycles = angle * F32(1.0 / (2.0 * math.pi))
    rest = cycles - jnp.round(cycles)
    square = rest * rest
    half_sine = horner(SIN_FINE, square) * rest
    return 1.0 - half_sine * half_sine, half_sine * horner(COS_FINE, square)


def unit_rows(angles):
    cos_all, sin_all = fine_cos_sin(angles)
    cos_polar, sin_polar = cos_all[0:1], sin_all[0:1]
    cos_azimuth, sin_azimuth = cos_all[1:2], sin_all[1:2]
    return sin_polar * cos_azimuth, sin_polar * sin_azimuth, cos_polar


def three_parts(value):
    first = value.astype(BF).astype(F32)
    second = (value - first).astype(BF).astype(F32)
    return first, second, value - first - second


def body(
    total_patches,
    angles_ref, positions_ref, normals_ref, areas_ref, pressure_hbm, velocity_hbm, targets_hbm,
    responses_ref, grads_ref,
    pressure_ref, velocity_ref, targets_t, targets_ref, angle_rows, angle_cols, angle_perm, split_t, split_x, t_rows, t_cols, t_lhs, x_rhs, face_rows, weights,
    cos_a, sin_a, cos_b, sin_b,
    part_send, part_recv, part_own, row_own, row_send, row_recv, res_all, acc,
    half_send, half_recv, quarter_own, quarter_send, quarter_recv, grad_all,
    local_sem, a_send, a_recv, b_send, b_recv, d_send, d_recv,
    e_send, e_recv,
    g_send, g_recv, h_send, h_recv, k_send, k_recv, m_send, m_recv,
):
    dir_index = lax.axis_index("dir")
    surf_index = lax.axis_index("surf")
    x, core = dir_index // 2, lax.rem(dir_index, 2)
    y, z = surf_index // NZ, lax.rem(surf_index, NZ)
    patches = positions_ref.shape[1]

    def at_y(e):
        return (dir_index, lax.rem(y + e, NY) * NZ + z)

    def at_z(e):
        return (dir_index, y * NZ + lax.rem(z + e, NZ))

    def at_dir(ex, ec):
        return (lax.rem(x + ex, NX) * 2 + lax.rem(core + ec, 2), surf_index)

    group = [(ex, 0) for ex in range(1, NX)] + [(0, 1)]
    barrier = pltpu.get_barrier_semaphore()
    for e in range(1, NY):
        pl.semaphore_signal(barrier, inc=1, device_id=at_y(e), device_id_type=MESH)
    for e in range(1, NZ):
        pl.semaphore_signal(barrier, inc=1, device_id=at_z(e), device_id_type=MESH)
    for ex, ec in group:
        pl.semaphore_signal(barrier, inc=1, device_id=at_dir(ex, ec), device_id_type=MESH)

    own_rows = TILES * OWN
    fetch = pltpu.make_async_copy(
        targets_hbm.at[:, pl.ds(pl.multiple_of(surf_index * own_rows, own_rows), own_rows)],
        targets_t, local_sem.at[0],
    )
    fetch_p = pltpu.make_async_copy(pressure_hbm, pressure_ref, local_sem.at[1])
    fetch_v = pltpu.make_async_copy(velocity_hbm, velocity_ref, local_sem.at[2])
    fetch_p.start()
    fetch_v.start()
    fetch.start()

    angle_rows[...] = jnp.zeros_like(angle_rows)
    angle_rows[0:2, :] = angles_ref[...]
    angle_cols[...] = angle_rows[...].T
    for q in range(TILES):
        for owner in range(NY * NZ):
            begin, source = q * ROWS + owner * OWN, owner * own_rows + q * OWN
            angle_perm[begin : begin + OWN, :] = angle_cols[source : source + OWN, :]
    tx, ty, tz = unit_rows(angle_perm[...].T)
    split_t[...] = jnp.zeros_like(split_t)
    split_x[...] = jnp.zeros_like(split_x)
    t_rows[...] = jnp.zeros_like(t_rows)
    for k, row in enumerate((tx, ty, tz)):
        t_rows[k : k + 1, :] = row
        first, second, third = three_parts(row)
        for at, part in enumerate((first, first, second, second, first, third)):
            split_t[3 * at + k : 3 * at + k + 1, :] = part
        first, second, third = three_parts(positions_ref[k : k + 1, :] * F32(0.5 / math.pi))
        for at, part in enumerate((first, second, first, second, third, first)):
            split_x[3 * at + k : 3 * at + k + 1, :] = part
    x_rhs[...] = split_x[...].astype(BF)
    t_lhs[...] = split_t[...].T.astype(BF)
    t_cols[...] = t_rows[...].T

    face_rows[...] = jnp.zeros_like(face_rows)
    for at in range(areas_ref.shape[0]):
        face_rows[3:4, 128 * at : 128 * (at + 1)] = areas_ref[at : at + 1, :]
    scale_row = face_rows[3:4, :] * F32(1.0 / math.sqrt(total_patches))
    for k, row in enumerate(unit_rows(normals_ref[...])):
        face_rows[k : k + 1, :] = row
    face_rows[3:4, :] = scale_row
    face_cols = face_rows[...].T
    scale_col = face_cols[:, 3:4]
    fetch_p.wait()
    fetch_v.wait()
    weighted_p = (pressure_ref[...].astype(F32) * scale_col).astype(BF).astype(F32)
    weighted_v = (velocity_ref[...].astype(F32) * scale_col).astype(BF).astype(F32)
    cases = weighted_p.shape[1] // 2
    for k in range(4):
        source = weighted_v if k == 0 else weighted_p * face_cols[:, k - 1 : k]
        turned = jnp.concatenate([source[:, cases:], -source[:, :cases]], axis=1)
        columns = slice(k * 2 * cases, (k + 1) * 2 * cases)
        weights[0:patches, columns] = source.astype(BF)
        weights[patches : 2 * patches, columns] = turned.astype(BF)
    acc[...] = jnp.zeros_like(acc)

    def sub_row(q, j):
        return pl.multiple_of(q * ROWS + lax.rem(y + DELTAS[j], NY) * SUB, SUB)

    def trig_piece(q, j, cos_ref, sin_ref, slot, begin, count):
        angle = jnp.dot(
            t_lhs[pl.ds(sub_row(q, j) + begin, count), :], x_rhs[...], preferred_element_type=F32
        )
        cosine, sine = cos_sin(angle)
        at = pl.multiple_of(slot * SUB + begin, count)
        cos_ref[pl.ds(at, count), :] = cosine.astype(BF)
        sin_ref[pl.ds(at, count), :] = sine.astype(BF)

    quarter = SUB // 4

    def forward_step(q, j, after=None):
        def make(piece):
            if after is not None:
                tq, tj, slot = after
                tc, ts = (cos_a, sin_a) if tj % 2 == 0 else (cos_b, sin_b)
                trig_piece(tq, tj, tc, ts, slot, piece * quarter, quarter)

        mc, ms = (cos_a, sin_a) if j % 2 == 0 else (cos_b, sin_b)
        rows = pl.ds(pl.multiple_of((2 * q + j // 2) * SUB, SUB), SUB)
        halves = []
        for h in range(2):
            columns = slice(4 * cases * h, 4 * cases * (h + 1))
            g = jnp.dot(mc[rows, :], weights[0:patches, columns], preferred_element_type=F32)
            make(2 * h)
            g = g + jnp.dot(
                ms[rows, :], weights[patches : 2 * patches, columns], preferred_element_type=F32
            )
            make(2 * h + 1)
            halves.append(g)
        t_at = t_cols[pl.ds(sub_row(q, j), SUB), :]
        lo, hi = halves
        return (
            lo[:, : 2 * cases]
            + t_at[:, 0:1] * lo[:, 2 * cases :]
            + t_at[:, 1:2] * hi[:, : 2 * cases]
            + t_at[:, 2:3] * hi[:, 2 * cases :]
        )

    def a_rows(q, e):
        return pl.ds(pl.multiple_of((q * (NY - 1) + e - 1) * SUB, SUB), SUB)

    def a_copy(q, e):
        return pltpu.make_async_remote_copy(
            src_ref=part_send.at[a_rows(q, e)], dst_ref=part_recv.at[a_rows(q, e)],
            send_sem=a_send.at[q * (NY - 1) + e - 1], recv_sem=a_recv.at[q * (NY - 1) + e - 1],
            device_id=at_y(e), device_id_type=MESH,
        )

    def b_copy(q, e):
        return pltpu.make_async_remote_copy(
            src_ref=row_send.at[pl.ds(pl.multiple_of(q * SUB + lax.rem(z + e, NZ) * OWN, OWN), OWN)],
            dst_ref=row_recv.at[pl.ds(pl.multiple_of((q * (NZ - 1) + e - 1) * OWN, OWN), OWN)],
            send_sem=b_send.at[q * (NZ - 1) + e - 1], recv_sem=b_recv.at[q * (NZ - 1) + e - 1],
            device_id=at_z(e), device_id_type=MESH,
        )

    def d_copy(q, e, came=False):
        source = lax.rem(z + NZ - e, NZ) if came else z
        rows = pl.ds(pl.multiple_of(q * ROWS + OURS * SUB + source * OWN, OWN), OWN)
        return pltpu.make_async_remote_copy(
            src_ref=res_all.at[rows], dst_ref=res_all.at[rows],
            send_sem=d_send.at[q * (NZ - 1) + e - 1], recv_sem=d_recv.at[q * (NZ - 1) + e - 1],
            device_id=at_z(e), device_id_type=MESH,
        )

    def e_copy(q, e):
        return pltpu.make_async_remote_copy(
            src_ref=res_all.at[pl.ds(pl.multiple_of(q * ROWS + OURS * SUB, SUB), SUB)],
            dst_ref=res_all.at[pl.ds(pl.multiple_of(q * ROWS + SLOT_OF_SEND[e] * SUB, SUB), SUB)],
            send_sem=e_send.at[q * (NY - 1) + e - 1], recv_sem=e_recv.at[q * (NY - 1) + e - 1],
            device_id=at_y(e), device_id_type=MESH,
        )

    def step_0(q):
        part_send[a_rows(q, DELTAS[0]), :] = forward_step(q, 0, (q, 1, 2 * q)).astype(BF)

    def step_1(q):
        part_send[a_rows(q, DELTAS[1]), :] = forward_step(q, 1, (q, 2, 2 * q + 1)).astype(BF)

        @pl.when(q == 0)
        def _():
            pl.semaphore_wait(barrier, (NY - 1) + (NZ - 1) + len(group))

        a_copy(q, DELTAS[0]).start()
        a_copy(q, DELTAS[1]).start()

    def step_2(q):
        part_send[a_rows(q, DELTAS[2]), :] = forward_step(q, 2, (q, 3, 2 * q + 1)).astype(BF)
        a_copy(q, DELTAS[2]).start()

    def step_3(q):
        rows = pl.ds(pl.multiple_of(q * SUB, SUB), SUB)

        @pl.when(q < TILES - 1)
        def _():
            part_own[rows, :] = forward_step(q, 3, (q + 1, 0, 2 * q + 2))

        @pl.when(q == TILES - 1)
        def _():
            part_own[rows, :] = forward_step(q, 3)

    def sum_over_y(q):
        rows = pl.ds(pl.multiple_of(q * SUB, SUB), SUB)
        total = part_own[rows, :]
        for e in range(1, NY):
            a_copy(q, e).wait_recv()
        for e in range(1, NY):
            total = total + part_recv[a_rows(q, e), :].astype(F32)
        row_own[rows, :] = total
        row_send[rows, :] = total.astype(BF)
        for e in FAR_FIRST:
            b_copy(q, e).start()

    def make_residual(q):
        total = row_own[pl.ds(pl.multiple_of(q * SUB + z * OWN, OWN), OWN), :]
        for e in range(1, NZ):
            b_copy(q, e).wait_recv()
        for e in range(1, NZ):
            at = pl.multiple_of((q * (NZ - 1) + e - 1) * OWN, OWN)
            total = total + row_recv[pl.ds(at, OWN), :].astype(F32)
        real, imag = -total[:, cases:], total[:, :cases]
        out_rows = pl.ds(pl.multiple_of(q * OWN, OWN), OWN)
        responses_ref[out_rows, :] = jnp.concatenate([real, imag], axis=1)
        magnitude = jnp.sqrt(real * real + imag * imag)
        weight = (magnitude - targets_ref[out_rows, :]) / jnp.maximum(magnitude, FLOOR)
        residual = jnp.concatenate([weight * real, weight * imag], axis=1).astype(BF)
        res_all[pl.ds(pl.multiple_of(q * ROWS + OURS * SUB + z * OWN, OWN), OWN), :] = residual
        for e in FAR_FIRST:
            d_copy(q, e).start()

    def share_over_y(q):
        for e in range(1, NZ):
            d_copy(q, e, came=True).wait_recv()
        for e in (2, 1, 3):
            e_copy(q, e).start()

    def adjoint_sides(q, parity):
        pieces, t_pieces = [], []
        for j in (parity, parity + 2):
            at = pl.multiple_of(q * ROWS + j * SUB, SUB)
            pieces.append(res_all[pl.ds(at, SUB), :].astype(F32))
            t_pieces.append(t_rows[:, pl.ds(sub_row(q, j), SUB)])
        turned = jnp.concatenate(pieces, axis=0).T
        t_at = jnp.concatenate(t_pieces, axis=1)
        swapped = jnp.concatenate([turned[cases:], -turned[:cases]], axis=0)
        with_cos, with_sin = [swapped.astype(BF)], [turned.astype(BF)]
        for k in range(3):
            with_cos.append((swapped * t_at[k : k + 1, :]).astype(BF))
            with_sin.append((turned * t_at[k : k + 1, :]).astype(BF))
        return jnp.concatenate(with_cos, axis=0), jnp.concatenate(with_sin, axis=0)

    def adjoint_add(q, parity, sides, columns):
        cos_ref, sin_ref = ((cos_a, sin_a), (cos_b, sin_b))[parity]
        rows = pl.ds(pl.multiple_of(q * 2 * SUB, 2 * SUB), 2 * SUB)
        acc[:, columns] += jnp.dot(
            sides[0], cos_ref[rows, columns], preferred_element_type=F32
        ) + jnp.dot(sides[1], sin_ref[rows, columns], preferred_element_type=F32)

    first_sends = [e for e in SLOT_OF_SEND if SLOT_OF_SEND[e] % 2 == 1]
    other_sends = [e for e in SLOT_OF_SEND if SLOT_OF_SEND[e] % 2 == 0]

    def adjoint_tile(q):
        for parity, sends in ((1, first_sends), (0, other_sends)):
            for e in sends:
                e_copy(q, e).wait_recv()
            adjoint_add(q, parity, adjoint_sides(q, parity), slice(0, patches))

    for begin in range(0, SUB, quarter):
        trig_piece(0, 0, cos_a, sin_a, 0, begin, quarter)
    fetch.wait()
    targets_ref[...] = targets_t[...].T

    def step(it, carry):
        def when(work, lag):
            inside = jnp.logical_and(it >= lag, it < TILES + lag)
            pl.when(inside)(lambda: work(it - lag))

        when(step_0, 0)
        when(step_1, 0)
        when(make_residual, 3)
        when(step_2, 0)
        when(step_3, 0)
        when(sum_over_y, 1)
        when(share_over_y, 4)
        pl.when(it >= 6)(lambda: adjoint_tile(it - 6))
        return carry

    lax.fori_loop(0, TILES + 5, step, 0)

    half = 2 * cases
    share = half // NX
    cuts = (slice(0, 512), slice(512, patches))
    last = TILES - 1

    def gradient(which, columns):
        if which == 0:
            return acc[0:half, columns] * scale_row[:, columns]
        total = acc[half : 2 * half, columns] * face_rows[0:1, columns]
        for k in range(1, 3):
            begin = (k + 1) * half
            total = total + acc[begin : begin + half, columns] * face_rows[k : k + 1, columns]
        return total * scale_row[:, columns]

    def g_copy(n):
        return pltpu.make_async_remote_copy(
            src_ref=half_send.at[:, cuts[n]], dst_ref=half_recv.at[:, cuts[n]],
            send_sem=g_send.at[n], recv_sem=g_recv.at[n],
            device_id=at_dir(0, 1), device_id_type=MESH,
        )

    def h_copy(n, e):
        source = pl.ds(pl.multiple_of(lax.rem(x + e, NX) * share, share), share)
        return pltpu.make_async_remote_copy(
            src_ref=quarter_send.at[source, cuts[n]],
            dst_ref=quarter_recv.at[pl.ds((e - 1) * share, share), cuts[n]],
            send_sem=h_send.at[3 * n + e - 1], recv_sem=h_recv.at[3 * n + e - 1],
            device_id=at_dir(e, 0), device_id_type=MESH,
        )

    def place(ex, ec):
        at = lax.rem(core + ec, 2) * half + lax.rem(x + NX - ex, NX) * share
        return pl.ds(pl.multiple_of(at, share), share)

    def k_copy(n, e, came=False):
        rows = place(e, 0) if came else place(0, 0)
        return pltpu.make_async_remote_copy(
            src_ref=grad_all.at[rows, cuts[n]], dst_ref=grad_all.at[rows, cuts[n]],
            send_sem=k_send.at[3 * n + e - 1], recv_sem=k_recv.at[3 * n + e - 1],
            device_id=at_dir(e, 0), device_id_type=MESH,
        )

    def m_copy(n, e, came=False):
        rows = place(e, 1) if came else place(e, 0)
        return pltpu.make_async_remote_copy(
            src_ref=grad_all.at[rows, cuts[n]], dst_ref=grad_all.at[rows, cuts[n]],
            send_sem=m_send.at[NX * n + e], recv_sem=m_recv.at[NX * n + e],
            device_id=at_dir(0, 1), device_id_type=MESH,
        )

    for e in first_sends:
        e_copy(last, e).wait_recv()
    adjoint_add(last, 1, adjoint_sides(last, 1), slice(0, patches))
    for e in other_sends:
        e_copy(last, e).wait_recv()
    sides = adjoint_sides(last, 0)
    for n, columns in enumerate(cuts):
        adjoint_add(last, 0, sides, columns)
        for which in range(2):
            grad = gradient(which, columns)

            @pl.when(core == which)
            def _():
                quarter_own[:, columns] = grad

            @pl.when(core != which)
            def _():
                half_send[:, columns] = grad.astype(BF)

        g_copy(n).start()
    def drain(q, carry):
        for e in range(1, NY):
            a_copy(q, e).wait_send()
            e_copy(q, e).wait_send()
        for e in range(1, NZ):
            b_copy(q, e).wait_send()
            d_copy(q, e).wait_send()
        return carry

    for n, columns in enumerate(cuts):
        g_copy(n).wait_recv()
        chip = quarter_own[:, columns] + half_recv[:, columns].astype(F32)
        quarter_own[:, columns] = chip
        quarter_send[:, columns] = chip.astype(BF)
        for e in (2, 1, 3):
            h_copy(n, e).start()
    lax.fori_loop(0, TILES, drain, 0)
    for n, columns in enumerate(cuts):
        total = quarter_own[pl.ds(pl.multiple_of(x * share, share), share), columns]
        for e in range(1, NX):
            h_copy(n, e).wait_recv()
        for e in range(1, NX):
            total = total + quarter_recv[(e - 1) * share : e * share, columns].astype(F32)
        grad_all[place(0, 0), columns] = total.astype(BF)
        for e in (2, 1, 3):
            k_copy(n, e).start()
        m_copy(n, 0).start()
    for n in range(2):
        g_copy(n).wait_send()
        for e in range(1, NX):
            h_copy(n, e).wait_send()
    for n in range(2):
        for e in (1, 3, 2):
            k_copy(n, e, came=True).wait_recv()
            m_copy(n, e).start()
    for n in range(2):
        for e in range(1, NX):
            k_copy(n, e).wait_send()
        for e in range(NX):
            m_copy(n, e, came=True).wait_recv()
    grads_ref[...] = grad_all[...]
    for n in range(2):
        for e in range(NX):
            m_copy(n, e).wait_send()


def finish(responses_ref, grads_ref, out_ref, grad_p_ref, grad_v_ref):
    half = grads_ref.shape[0] // 2
    out_ref[...] = responses_ref[...]
    grad_v_ref[...] = grads_ref[0:half, :].astype(F32).T
    grad_p_ref[...] = grads_ref[half : 2 * half, :].astype(F32).T


def shards(direction_angles, positions, normal_angles, areas, pressure, velocity, targets):
    cases = targets.shape[1]
    patches = positions.shape[1]
    dirs = direction_angles.shape[1]
    total_patches = patches * lax.axis_size("surf")
    owners = NY * NZ
    vmem = pl.BlockSpec(memory_space=pltpu.VMEM)
    half = 2 * cases
    dma = pltpu.SemaphoreType.DMA
    slots = 2 * TILES
    responses, grads = pl.pallas_call(
        functools.partial(body, total_patches),
        out_shape=(
            jax.ShapeDtypeStruct((dirs // owners, half), F32),
            jax.ShapeDtypeStruct((2 * half, patches), BF),
        ),
        in_specs=[vmem] * 4 + [pl.BlockSpec(memory_space=pl.ANY)] * 3,
        out_specs=(vmem, vmem),
        scratch_shapes=[
            pltpu.VMEM((patches, half), BF),
            pltpu.VMEM((patches, half), BF),
            pltpu.VMEM((cases, TILES * OWN), F32),
            pltpu.VMEM((TILES * OWN, cases), F32),
            pltpu.VMEM((8, dirs), F32),
            pltpu.VMEM((dirs, 8), F32),
            pltpu.VMEM((dirs, 8), F32),
            pltpu.VMEM((32, dirs), F32),
            pltpu.VMEM((32, patches), F32),
            pltpu.VMEM((8, dirs), F32),
            pltpu.VMEM((dirs, 8), F32),
            pltpu.VMEM((dirs, 32), BF),
            pltpu.VMEM((32, patches), BF),
            pltpu.VMEM((8, patches), F32),
            pltpu.VMEM((2 * patches, 4 * half), BF),
            pltpu.VMEM((slots * SUB, patches), BF),
            pltpu.VMEM((slots * SUB, patches), BF),
            pltpu.VMEM((slots * SUB, patches), BF),
            pltpu.VMEM((slots * SUB, patches), BF),
            pltpu.VMEM((TILES * (NY - 1) * SUB, half), BF),
            pltpu.VMEM((TILES * (NY - 1) * SUB, half), BF),
            pltpu.VMEM((TILES * SUB, half), F32),
            pltpu.VMEM((TILES * SUB, half), F32),
            pltpu.VMEM((TILES * SUB, half), BF),
            pltpu.VMEM((TILES * (NZ - 1) * OWN, half), BF),
            pltpu.VMEM((TILES * ROWS, half), BF),
            pltpu.VMEM((4 * half, patches), F32),
            pltpu.VMEM((half, patches), BF),
            pltpu.VMEM((half, patches), BF),
            pltpu.VMEM((half, patches), F32),
            pltpu.VMEM((half, patches), BF),
            pltpu.VMEM((half // NX * (NX - 1), patches), BF),
            pltpu.VMEM((2 * half, patches), BF),
            dma((3,)),
            dma((TILES * (NY - 1),)), dma((TILES * (NY - 1),)),
            dma((TILES * (NZ - 1),)), dma((TILES * (NZ - 1),)),
            dma((TILES * (NZ - 1),)), dma((TILES * (NZ - 1),)),
            dma((TILES * (NY - 1),)), dma((TILES * (NY - 1),)),
            dma((2,)), dma((2,)),
            dma((2 * (NX - 1),)), dma((2 * (NX - 1),)),
            dma((2 * (NX - 1),)), dma((2 * (NX - 1),)),
            dma((2 * NX,)), dma((2 * NX,)),
        ],
        compiler_params=pltpu.CompilerParams(
            collective_id=0, has_side_effects=True, vmem_limit_bytes=56 * 2**20
        ),
    )(
        direction_angles, positions, normal_angles, areas.reshape(patches // 128, 128),
        pressure, velocity, targets.T,
    )
    return pl.pallas_call(
        finish,
        out_shape=(
            jax.ShapeDtypeStruct((dirs // owners, half), F32),
            jax.ShapeDtypeStruct((patches, half), F32),
            jax.ShapeDtypeStruct((patches, half), F32),
        ),
        in_specs=[vmem] * 2,
        out_specs=(vmem, vmem, vmem),
    )(responses, grads)


def solution(mesh):
    in_specs = (
        P(None, "dir"),
        P(None, "surf"),
        P(None, "surf"),
        P("surf"),
        P("surf", None),
        P("surf", None),
        P("dir", None),
    )
    out_specs = (P(("dir", "surf"), None), P("surf", None), P("surf", None))
    return jax.shard_map(shards, mesh=mesh, in_specs=in_specs, out_specs=out_specs, check_vma=False)
```

```python
import functools
import math

import jax
import jax.numpy as jnp
from jax import lax
from jax.experimental import pallas as pl
from jax.experimental.pallas import tpu as pltpu
from jax.sharding import PartitionSpec as P

MESH = pl.DeviceIdType.MESH
BF = jnp.bfloat16
F32 = jnp.float32
FLOOR = 0.5

TILES = 4
NY, NZ, NX = 4, 8, 4
OWN = 32
SUB = NZ * OWN
ROWS = NY * SUB
DELTAS = (2, 1, 3, 0)
FAR_FIRST = (4, 3, 5, 2, 6, 1, 7)
OURS = 3
SLOT_OF_SEND = {1: 2, 2: 0, 3: 1}

ROOT2 = math.sqrt(2.0)
SIN_HALF = [c * ROOT2 for c in (3.14158198, -5.1671413, 2.54188707, -0.55460885)]
SIN_FINE = [c * ROOT2 for c in (3.14159258, -5.16770687, 2.55003119, -0.59804419, 0.07721839)]
COS_FINE = [c * ROOT2 for c in (0.99999995, -4.93479283, 4.05841135, -1.33187657, 0.21968961)]


def horner(coefficients, square):
    value = coefficients[-1]
    for coefficient in coefficients[-2::-1]:
        value = value * square + coefficient
    return value


def cos_sin(cycles):
    rest = cycles - jnp.round(cycles)
    half_sine = horner(SIN_HALF, rest * rest) * rest
    double = half_sine * half_sine
    left = jnp.maximum(2.0 - double, 1e-20)
    return 1.0 - double, half_sine * (left * lax.rsqrt(left))


def fine_cos_sin(angle):
    cycles = angle * F32(1.0 / (2.0 * math.pi))
    rest = cycles - jnp.round(cycles)
    square = rest * rest
    half_sine = horner(SIN_FINE, square) * rest
    return 1.0 - half_sine * half_sine, half_sine * horner(COS_FINE, square)


def unit_rows(angles):
    cos_all, sin_all = fine_cos_sin(angles)
    cos_polar, sin_polar = cos_all[0:1], sin_all[0:1]
    cos_azimuth, sin_azimuth = cos_all[1:2], sin_all[1:2]
    return sin_polar * cos_azimuth, sin_polar * sin_azimuth, cos_polar


def three_parts(value):
    first = value.astype(BF).astype(F32)
    second = (value - first).astype(BF).astype(F32)
    return first, second, value - first - second


def body(
    total_patches,
    angles_ref, positions_ref, normals_ref, areas_ref, pressure_hbm, velocity_hbm, targets_hbm,
    responses_ref, grads_ref,
    pressure_ref, velocity_ref, targets_t, targets_ref, angle_rows, angle_cols, angle_perm, split_t, split_x, t_rows, t_cols, t_lhs, x_rhs, face_rows, weights,
    cos_a, sin_a, cos_b, sin_b,
    part_send, part_recv, part_own, row_own, row_send, row_recv, res_all, acc,
    half_send, half_recv, quarter_own, quarter_send, quarter_recv, grad_all,
    local_sem, a_send, a_recv, b_send, b_recv, d_send, d_recv,
    e_send, e_recv,
    g_send, g_recv, h_send, h_recv, k_send, k_recv, m_send, m_recv,
):
    dir_index = lax.axis_index("dir")
    surf_index = lax.axis_index("surf")
    x, core = dir_index // 2, lax.rem(dir_index, 2)
    y, z = surf_index // NZ, lax.rem(surf_index, NZ)
    patches = positions_ref.shape[1]

    def at_y(e):
        return (dir_index, lax.rem(y + e, NY) * NZ + z)

    def at_z(e):
        return (dir_index, y * NZ + lax.rem(z + e, NZ))

    def at_dir(ex, ec):
        return (lax.rem(x + ex, NX) * 2 + lax.rem(core + ec, 2), surf_index)

    group = [(ex, 0) for ex in range(1, NX)] + [(0, 1)]
    barrier = pltpu.get_barrier_semaphore()
    for e in range(1, NY):
        pl.semaphore_signal(barrier, inc=1, device_id=at_y(e), device_id_type=MESH)
    for e in range(1, NZ):
        pl.semaphore_signal(barrier, inc=1, device_id=at_z(e), device_id_type=MESH)
    for ex, ec in group:
        pl.semaphore_signal(barrier, inc=1, device_id=at_dir(ex, ec), device_id_type=MESH)

    own_rows = TILES * OWN
    fetch = pltpu.make_async_copy(
        targets_hbm.at[:, pl.ds(pl.multiple_of(surf_index * own_rows, own_rows), own_rows)],
        targets_t, local_sem.at[0],
    )
    fetch_p = pltpu.make_async_copy(pressure_hbm, pressure_ref, local_sem.at[1])
    fetch_v = pltpu.make_async_copy(velocity_hbm, velocity_ref, local_sem.at[2])
    fetch_p.start()
    fetch_v.start()
    fetch.start()

    angle_rows[...] = jnp.zeros_like(angle_rows)
    angle_rows[0:2, :] = angles_ref[...]
    angle_cols[...] = angle_rows[...].T
    for q in range(TILES):
        for owner in range(NY * NZ):
            begin, source = q * ROWS + owner * OWN, owner * own_rows + q * OWN
            angle_perm[begin : begin + OWN, :] = angle_cols[source : source + OWN, :]
    tx, ty, tz = unit_rows(angle_perm[...].T)
    split_t[...] = jnp.zeros_like(split_t)
    split_x[...] = jnp.zeros_like(split_x)
    t_rows[...] = jnp.zeros_like(t_rows)
    for k, row in enumerate((tx, ty, tz)):
        t_rows[k : k + 1, :] = row
        first, second, third = three_parts(row)
        for at, part in enumerate((first, first, second, second, first, third)):
            split_t[3 * at + k : 3 * at + k + 1, :] = part
        first, second, third = three_parts(positions_ref[k : k + 1, :] * F32(0.5 / math.pi))
        for at, part in enumerate((first, second, first, second, third, first)):
            split_x[3 * at + k : 3 * at + k + 1, :] = part
    x_rhs[...] = split_x[...].astype(BF)
    t_lhs[...] = split_t[...].T.astype(BF)
    t_cols[...] = t_rows[...].T

    face_rows[...] = jnp.zeros_like(face_rows)
    for at in range(areas_ref.shape[0]):
        face_rows[3:4, 128 * at : 128 * (at + 1)] = areas_ref[at : at + 1, :]
    scale_row = face_rows[3:4, :] * F32(1.0 / math.sqrt(total_patches))
    for k, row in enumerate(unit_rows(normals_ref[...])):
        face_rows[k : k + 1, :] = row
    face_rows[3:4, :] = scale_row
    face_cols = face_rows[...].T
    scale_col = face_cols[:, 3:4]
    fetch_p.wait()
    fetch_v.wait()
    weighted_p = (pressure_ref[...].astype(F32) * scale_col).astype(BF).astype(F32)
    weighted_v = (velocity_ref[...].astype(F32) * scale_col).astype(BF).astype(F32)
    cases = weighted_p.shape[1] // 2
    for k in range(4):
        source = weighted_v if k == 0 else weighted_p * face_cols[:, k - 1 : k]
        turned = jnp.concatenate([source[:, cases:], -source[:, :cases]], axis=1)
        columns = slice(k * 2 * cases, (k + 1) * 2 * cases)
        weights[0:patches, columns] = source.astype(BF)
        weights[patches : 2 * patches, columns] = turned.astype(BF)
    acc[...] = jnp.zeros_like(acc)

    def sub_row(q, j):
        return pl.multiple_of(q * ROWS + lax.rem(y + DELTAS[j], NY) * SUB, SUB)

    def trig_piece(q, j, cos_ref, sin_ref, slot, begin, count):
        angle = jnp.dot(
            t_lhs[pl.ds(sub_row(q, j) + begin, count), :], x_rhs[...], preferred_element_type=F32
        )
        cosine, sine = cos_sin(angle)
        at = pl.multiple_of(slot * SUB + begin, count)
        cos_ref[pl.ds(at, count), :] = cosine.astype(BF)
        sin_ref[pl.ds(at, count), :] = sine.astype(BF)

    quarter = SUB // 4

    def forward_step(q, j, after=None):
        def make(piece):
            if after is not None:
                tq, tj, slot = after
                tc, ts = (cos_a, sin_a) if tj % 2 == 0 else (cos_b, sin_b)
                trig_piece(tq, tj, tc, ts, slot, piece * quarter, quarter)

        mc, ms = (cos_a, sin_a) if j % 2 == 0 else (cos_b, sin_b)
        rows = pl.ds(pl.multiple_of((2 * q + j // 2) * SUB, SUB), SUB)
        halves = []
        for h in range(2):
            columns = slice(4 * cases * h, 4 * cases * (h + 1))
            g = jnp.dot(mc[rows, :], weights[0:patches, columns], preferred_element_type=F32)
            make(2 * h)
            g = g + jnp.dot(
                ms[rows, :], weights[patches : 2 * patches, columns], preferred_element_type=F32
            )
            make(2 * h + 1)
            halves.append(g)
        t_at = t_cols[pl.ds(sub_row(q, j), SUB), :]
        lo, hi = halves
        return (
            lo[:, : 2 * cases]
            + t_at[:, 0:1] * lo[:, 2 * cases :]
            + t_at[:, 1:2] * hi[:, : 2 * cases]
            + t_at[:, 2:3] * hi[:, 2 * cases :]
        )

    def a_rows(q, e):
        return pl.ds(pl.multiple_of((q * (NY - 1) + e - 1) * SUB, SUB), SUB)

    def a_copy(q, e):
        return pltpu.make_async_remote_copy(
            src_ref=part_send.at[a_rows(q, e)], dst_ref=part_recv.at[a_rows(q, e)],
            send_sem=a_send.at[q * (NY - 1) + e - 1], recv_sem=a_recv.at[q * (NY - 1) + e - 1],
            device_id=at_y(e), device_id_type=MESH,
        )

    def b_copy(q, e):
        return pltpu.make_async_remote_copy(
            src_ref=row_send.at[pl.ds(pl.multiple_of(q * SUB + lax.rem(z + e, NZ) * OWN, OWN), OWN)],
            dst_ref=row_recv.at[pl.ds(pl.multiple_of((q * (NZ - 1) + e - 1) * OWN, OWN), OWN)],
            send_sem=b_send.at[q * (NZ - 1) + e - 1], recv_sem=b_recv.at[q * (NZ - 1) + e - 1],
            device_id=at_z(e), device_id_type=MESH,
        )

    def d_copy(q, e, came=False):
        source = lax.rem(z + NZ - e, NZ) if came else z
        rows = pl.ds(pl.multiple_of(q * ROWS + OURS * SUB + source * OWN, OWN), OWN)
        return pltpu.make_async_remote_copy(
            src_ref=res_all.at[rows], dst_ref=res_all.at[rows],
            send_sem=d_send.at[q * (NZ - 1) + e - 1], recv_sem=d_recv.at[q * (NZ - 1) + e - 1],
            device_id=at_z(e), device_id_type=MESH,
        )

    def e_copy(q, e):
        return pltpu.make_async_remote_copy(
            src_ref=res_all.at[pl.ds(pl.multiple_of(q * ROWS + OURS * SUB, SUB), SUB)],
            dst_ref=res_all.at[pl.ds(pl.multiple_of(q * ROWS + SLOT_OF_SEND[e] * SUB, SUB), SUB)],
            send_sem=e_send.at[q * (NY - 1) + e - 1], recv_sem=e_recv.at[q * (NY - 1) + e - 1],
            device_id=at_y(e), device_id_type=MESH,
        )

    def step_0(q):
        part_send[a_rows(q, DELTAS[0]), :] = forward_step(q, 0, (q, 1, 2 * q)).astype(BF)

    def step_1(q):
        part_send[a_rows(q, DELTAS[1]), :] = forward_step(q, 1, (q, 2, 2 * q + 1)).astype(BF)

        @pl.when(q == 0)
        def _():
            pl.semaphore_wait(barrier, (NY - 1) + (NZ - 1) + len(group))

        a_copy(q, DELTAS[0]).start()
        a_copy(q, DELTAS[1]).start()

    def step_2(q):
        part_send[a_rows(q, DELTAS[2]), :] = forward_step(q, 2, (q, 3, 2 * q + 1)).astype(BF)
        a_copy(q, DELTAS[2]).start()

    def step_3(q):
        rows = pl.ds(pl.multiple_of(q * SUB, SUB), SUB)

        @pl.when(q < TILES - 1)
        def _():
            part_own[rows, :] = forward_step(q, 3, (q + 1, 0, 2 * q + 2))

        @pl.when(q == TILES - 1)
        def _():
            part_own[rows, :] = forward_step(q, 3)

    def sum_over_y(q):
        rows = pl.ds(pl.multiple_of(q * SUB, SUB), SUB)
        total = part_own[rows, :]
        for e in range(1, NY):
            a_copy(q, e).wait_recv()
        for e in range(1, NY):
            total = total + part_recv[a_rows(q, e), :].astype(F32)
        row_own[rows, :] = total
        row_send[rows, :] = total.astype(BF)
        for e in FAR_FIRST:
            b_copy(q, e).start()

    def make_residual(q):
        total = row_own[pl.ds(pl.multiple_of(q * SUB + z * OWN, OWN), OWN), :]
        for e in range(1, NZ):
            b_copy(q, e).wait_recv()
        for e in range(1, NZ):
            at = pl.multiple_of((q * (NZ - 1) + e - 1) * OWN, OWN)
            total = total + row_recv[pl.ds(at, OWN), :].astype(F32)
        real, imag = -total[:, cases:], total[:, :cases]
        out_rows = pl.ds(pl.multiple_of(q * OWN, OWN), OWN)
        responses_ref[out_rows, :] = jnp.concatenate([real, imag], axis=1)
        magnitude = jnp.sqrt(real * real + imag * imag)
        weight = (magnitude - targets_ref[out_rows, :]) / jnp.maximum(magnitude, FLOOR)
        residual = jnp.concatenate([weight * real, weight * imag], axis=1).astype(BF)
        res_all[pl.ds(pl.multiple_of(q * ROWS + OURS * SUB + z * OWN, OWN), OWN), :] = residual
        for e in FAR_FIRST:
            d_copy(q, e).start()

    def share_over_y(q):
        for e in range(1, NZ):
            d_copy(q, e, came=True).wait_recv()
        for e in (2, 1, 3):
            e_copy(q, e).start()

    def adjoint_sides(q, parity):
        pieces, t_pieces = [], []
        for j in (parity, parity + 2):
            at = pl.multiple_of(q * ROWS + j * SUB, SUB)
            pieces.append(res_all[pl.ds(at, SUB), :].astype(F32))
            t_pieces.append(t_rows[:, pl.ds(sub_row(q, j), SUB)])
        turned = jnp.concatenate(pieces, axis=0).T
        t_at = jnp.concatenate(t_pieces, axis=1)
        swapped = jnp.concatenate([turned[cases:], -turned[:cases]], axis=0)
        with_cos, with_sin = [swapped.astype(BF)], [turned.astype(BF)]
        for k in range(3):
            with_cos.append((swapped * t_at[k : k + 1, :]).astype(BF))
            with_sin.append((turned * t_at[k : k + 1, :]).astype(BF))
        return jnp.concatenate(with_cos, axis=0), jnp.concatenate(with_sin, axis=0)

    def adjoint_add(q, parity, sides, columns):
        cos_ref, sin_ref = ((cos_a, sin_a), (cos_b, sin_b))[parity]
        rows = pl.ds(pl.multiple_of(q * 2 * SUB, 2 * SUB), 2 * SUB)
        acc[:, columns] += jnp.dot(
            sides[0], cos_ref[rows, columns], preferred_element_type=F32
        ) + jnp.dot(sides[1], sin_ref[rows, columns], preferred_element_type=F32)

    first_sends = [e for e in SLOT_OF_SEND if SLOT_OF_SEND[e] % 2 == 1]
    other_sends = [e for e in SLOT_OF_SEND if SLOT_OF_SEND[e] % 2 == 0]

    def adjoint_tile(q):
        for parity, sends in ((1, first_sends), (0, other_sends)):
            for e in sends:
                e_copy(q, e).wait_recv()
            adjoint_add(q, parity, adjoint_sides(q, parity), slice(0, patches))

    for begin in range(0, SUB, quarter):
        trig_piece(0, 0, cos_a, sin_a, 0, begin, quarter)
    fetch.wait()
    targets_ref[...] = targets_t[...].T

    def step(it, carry):
        def when(work, lag):
            inside = jnp.logical_and(it >= lag, it < TILES + lag)
            pl.when(inside)(lambda: work(it - lag))

        when(step_0, 0)
        when(step_1, 0)
        when(make_residual, 3)
        when(step_2, 0)
        when(step_3, 0)
        when(sum_over_y, 1)
        when(share_over_y, 4)
        pl.when(it >= 6)(lambda: adjoint_tile(it - 6))
        return carry

    lax.fori_loop(0, TILES + 5, step, 0)

    half = 2 * cases
    share = half // NX
    cuts = (slice(0, 256), slice(256, patches))
    last = TILES - 1

    def gradient(which, columns):
        if which == 0:
            return acc[0:half, columns] * scale_row[:, columns]
        total = acc[half : 2 * half, columns] * face_rows[0:1, columns]
        for k in range(1, 3):
            begin = (k + 1) * half
            total = total + acc[begin : begin + half, columns] * face_rows[k : k + 1, columns]
        return total * scale_row[:, columns]

    def g_copy(n):
        return pltpu.make_async_remote_copy(
            src_ref=half_send.at[:, cuts[n]], dst_ref=half_recv.at[:, cuts[n]],
            send_sem=g_send.at[n], recv_sem=g_recv.at[n],
            device_id=at_dir(0, 1), device_id_type=MESH,
        )

    def h_copy(n, e):
        source = pl.ds(pl.multiple_of(lax.rem(x + e, NX) * share, share), share)
        return pltpu.make_async_remote_copy(
            src_ref=quarter_send.at[source, cuts[n]],
            dst_ref=quarter_recv.at[pl.ds((e - 1) * share, share), cuts[n]],
            send_sem=h_send.at[3 * n + e - 1], recv_sem=h_recv.at[3 * n + e - 1],
            device_id=at_dir(e, 0), device_id_type=MESH,
        )

    def place(ex, ec):
        at = lax.rem(core + ec, 2) * half + lax.rem(x + NX - ex, NX) * share
        return pl.ds(pl.multiple_of(at, share), share)

    def k_copy(n, e, came=False):
        rows = place(e, 0) if came else place(0, 0)
        return pltpu.make_async_remote_copy(
            src_ref=grad_all.at[rows, cuts[n]], dst_ref=grad_all.at[rows, cuts[n]],
            send_sem=k_send.at[3 * n + e - 1], recv_sem=k_recv.at[3 * n + e - 1],
            device_id=at_dir(e, 0), device_id_type=MESH,
        )

    def m_copy(n, e, came=False):
        rows = place(e, 1) if came else place(e, 0)
        return pltpu.make_async_remote_copy(
            src_ref=grad_all.at[rows, cuts[n]], dst_ref=grad_all.at[rows, cuts[n]],
            send_sem=m_send.at[NX * n + e], recv_sem=m_recv.at[NX * n + e],
            device_id=at_dir(0, 1), device_id_type=MESH,
        )

    for e in first_sends:
        e_copy(last, e).wait_recv()
    adjoint_add(last, 1, adjoint_sides(last, 1), slice(0, patches))
    for e in other_sends:
        e_copy(last, e).wait_recv()
    sides = adjoint_sides(last, 0)
    for n, columns in enumerate(cuts):
        adjoint_add(last, 0, sides, columns)
        for which in range(2):
            grad = gradient(which, columns)

            @pl.when(core == which)
            def _():
                quarter_own[:, columns] = grad

            @pl.when(core != which)
            def _():
                half_send[:, columns] = grad.astype(BF)

        g_copy(n).start()
    def drain(q, carry):
        for e in range(1, NY):
            a_copy(q, e).wait_send()
            e_copy(q, e).wait_send()
        for e in range(1, NZ):
            b_copy(q, e).wait_send()
            d_copy(q, e).wait_send()
        return carry

    for n, columns in enumerate(cuts):
        g_copy(n).wait_recv()
        chip = quarter_own[:, columns] + half_recv[:, columns].astype(F32)
        quarter_own[:, columns] = chip
        quarter_send[:, columns] = chip.astype(BF)
        for e in (2, 1, 3):
            h_copy(n, e).start()
    lax.fori_loop(0, TILES, drain, 0)
    for n, columns in enumerate(cuts):
        total = quarter_own[pl.ds(pl.multiple_of(x * share, share), share), columns]
        for e in range(1, NX):
            h_copy(n, e).wait_recv()
        for e in range(1, NX):
            total = total + quarter_recv[(e - 1) * share : e * share, columns].astype(F32)
        grad_all[place(0, 0), columns] = total.astype(BF)
        for e in (2, 1, 3):
            k_copy(n, e).start()
        m_copy(n, 0).start()
    for n in range(2):
        g_copy(n).wait_send()
        for e in range(1, NX):
            h_copy(n, e).wait_send()
    for n in range(2):
        for e in (1, 3, 2):
            k_copy(n, e, came=True).wait_recv()
            m_copy(n, e).start()
    for n in range(2):
        for e in range(1, NX):
            k_copy(n, e).wait_send()
        for e in range(NX):
            m_copy(n, e, came=True).wait_recv()
    grads_ref[...] = grad_all[...]
    for n in range(2):
        for e in range(NX):
            m_copy(n, e).wait_send()


def finish(responses_ref, grads_ref, out_ref, grad_p_ref, grad_v_ref):
    half = grads_ref.shape[0] // 2
    out_ref[...] = responses_ref[...]
    grad_v_ref[...] = grads_ref[0:half, :].astype(F32).T
    grad_p_ref[...] = grads_ref[half : 2 * half, :].astype(F32).T


def shards(direction_angles, positions, normal_angles, areas, pressure, velocity, targets):
    cases = targets.shape[1]
    patches = positions.shape[1]
    dirs = direction_angles.shape[1]
    total_patches = patches * lax.axis_size("surf")
    owners = NY * NZ
    vmem = pl.BlockSpec(memory_space=pltpu.VMEM)
    half = 2 * cases
    dma = pltpu.SemaphoreType.DMA
    slots = 2 * TILES
    responses, grads = pl.pallas_call(
        functools.partial(body, total_patches),
        out_shape=(
            jax.ShapeDtypeStruct((dirs // owners, half), F32),
            jax.ShapeDtypeStruct((2 * half, patches), BF),
        ),
        in_specs=[vmem] * 4 + [pl.BlockSpec(memory_space=pl.ANY)] * 3,
        out_specs=(vmem, vmem),
        scratch_shapes=[
            pltpu.VMEM((patches, half), BF),
            pltpu.VMEM((patches, half), BF),
            pltpu.VMEM((cases, TILES * OWN), F32),
            pltpu.VMEM((TILES * OWN, cases), F32),
            pltpu.VMEM((8, dirs), F32),
            pltpu.VMEM((dirs, 8), F32),
            pltpu.VMEM((dirs, 8), F32),
            pltpu.VMEM((32, dirs), F32),
            pltpu.VMEM((32, patches), F32),
            pltpu.VMEM((8, dirs), F32),
            pltpu.VMEM((dirs, 8), F32),
            pltpu.VMEM((dirs, 32), BF),
            pltpu.VMEM((32, patches), BF),
            pltpu.VMEM((8, patches), F32),
            pltpu.VMEM((2 * patches, 4 * half), BF),
            pltpu.VMEM((slots * SUB, patches), BF),
            pltpu.VMEM((slots * SUB, patches), BF),
            pltpu.VMEM((slots * SUB, patches), BF),
            pltpu.VMEM((slots * SUB, patches), BF),
            pltpu.VMEM((TILES * (NY - 1) * SUB, half), BF),
            pltpu.VMEM((TILES * (NY - 1) * SUB, half), BF),
            pltpu.VMEM((TILES * SUB, half), F32),
            pltpu.VMEM((TILES * SUB, half), F32),
            pltpu.VMEM((TILES * SUB, half), BF),
            pltpu.VMEM((TILES * (NZ - 1) * OWN, half), BF),
            pltpu.VMEM((TILES * ROWS, half), BF),
            pltpu.VMEM((4 * half, patches), F32),
            pltpu.VMEM((half, patches), BF),
            pltpu.VMEM((half, patches), BF),
            pltpu.VMEM((half, patches), F32),
            pltpu.VMEM((half, patches), BF),
            pltpu.VMEM((half // NX * (NX - 1), patches), BF),
            pltpu.VMEM((2 * half, patches), BF),
            dma((3,)),
            dma((TILES * (NY - 1),)), dma((TILES * (NY - 1),)),
            dma((TILES * (NZ - 1),)), dma((TILES * (NZ - 1),)),
            dma((TILES * (NZ - 1),)), dma((TILES * (NZ - 1),)),
            dma((TILES * (NY - 1),)), dma((TILES * (NY - 1),)),
            dma((2,)), dma((2,)),
            dma((2 * (NX - 1),)), dma((2 * (NX - 1),)),
            dma((2 * (NX - 1),)), dma((2 * (NX - 1),)),
            dma((2 * NX,)), dma((2 * NX,)),
        ],
        compiler_params=pltpu.CompilerParams(
            collective_id=0, has_side_effects=True, vmem_limit_bytes=56 * 2**20
        ),
    )(
        direction_angles, positions, normal_angles, areas.reshape(patches // 128, 128),
        pressure, velocity, targets.T,
    )
    return pl.pallas_call(
        finish,
        out_shape=(
            jax.ShapeDtypeStruct((dirs // owners, half), F32),
            jax.ShapeDtypeStruct((patches, half), F32),
            jax.ShapeDtypeStruct((patches, half), F32),
        ),
        in_specs=[vmem] * 2,
        out_specs=(vmem, vmem, vmem),
    )(responses, grads)


def solution(mesh):
    in_specs = (
        P(None, "dir"),
        P(None, "surf"),
        P(None, "surf"),
        P("surf"),
        P("surf", None),
        P("surf", None),
        P("dir", None),
    )
    out_specs = (P(("dir", "surf"), None), P("surf", None), P("surf", None))
    return jax.shard_map(shards, mesh=mesh, in_specs=in_specs, out_specs=out_specs, check_vma=False)
```
